128 devices in a mesh: plane: 16 (over x, z), height: 8 (over y, core).
Axes of the slice: x: 4, y: 4, z: 4, core: 2. Of those that a mesh axis runs over, the one named last changes fastest.
Arguments:
- points: bfloat16 [262144, 128], P(('plane', 'height')), may hold values from -6 to 6
- point_brick: int32 [262144, 1], P(('plane', 'height')), may hold values from 0 to 127; in each aligned block of 2048 rows (0 to 2047, 2048 to 4095, ...) at most 32 rows name the same one
- point_voxel: int32 [262144], P(('plane', 'height')), may hold values from 0 to 1023
- send_rows: int32 [16, 8, 4, 64], P('plane', 'height'), may hold values from 0 to 1023
- pair_in: int32 [16, 8, 26, 256], P('plane', 'height'), may hold values from 0 to 1280, as said below
- pair_out: int32 [16, 8, 26, 256], P('plane', 'height'), may hold values from 0 to 1024, as said below
- bev_cell: int32 [16, 8, 1024], P('plane', 'height'), may hold values from 0 to 4095
- conv_weight: bfloat16 [27, 128, 256], replicated, may hold values from -0.1875 to 0.1875
- head_weight: bfloat16 [9, 256, 128], replicated, may hold values from -0.125 to 0.125
- head_cot: bfloat16 [1024, 64, 128], P('plane'), may hold values from -0.0234375 to 0.0234375
Outputs:
- head_out: bfloat16 [1024, 64, 128], P(('plane', 'height'))
- conv_grad: float32 [27, 128, 256], replicated
- head_grad: float32 [9, 256, 128], replicated
The draws below stay inside these ranges and needn't reach their ends.
Inputs may be any that keep to these rules, and one draw needn't show every extreme that they name: `point_brick`: in the rows of one device no brick appears more than 32 times. `pair_in`: the value 1024 + 4 * 64 names the zero row and marks a padding pair. `pair_out`: the value 1024 marks a padding pair whose result is dropped.
All inputs are finite; a program needn't handle non-finite values.
Results may differ from the reference program's by a relative error of at most 0.017.
Values may be sent and summed in bfloat16 or wider, within the bound.
No kernel may reach another device: no remote copies, remote signals or barrier semaphores. Data moves between devices by JAX's collectives and lax.ppermute only.
A program may use at most 128 MiB of HBM per device.

```python
import math
import jax
import jax.numpy as jnp
import numpy as np
from jax import lax

C_PT = 128
C_OUT = 256
C_HEAD = 128
BX = 64
BY = 64
P_DEV = 2048
V = 1024
TILES = 16
LAYERS = 8
POINTS = 262144
CAP = 32
RIM = 64
PAIRS = 256
DEVICES = 128


def draw_pair_in(key, part):
    key = jax.random.fold_in(key, 11)
    first, second = jax.random.split(key)
    shape = (TILES, LAYERS, 26, PAIRS)
    chosen = jax.random.randint(first, shape, 0, V + 4 * RIM)
    padding = jax.random.randint(second, shape, 0, 4) == 0
    return jnp.where(padding, V + 4 * RIM, chosen).astype(jnp.int32)


def draw_pair_out(key, part):
    key = jax.random.fold_in(key, 23)
    first, second = jax.random.split(key)
    shape = (TILES, LAYERS, 26, PAIRS)
    chosen = jax.random.randint(first, shape, 0, V)
    padding = jax.random.randint(second, shape, 0, 4) == 0
    return jnp.where(padding, V, chosen).astype(jnp.int32)


def plant(entries, rng, low, largest):
    extent = entries.shape
    index_at = [jax.random.randint(jax.random.fold_in(rng, axis), (), 0, extent[axis]) for axis in range(len(extent))]
    entries = entries.at[tuple(index_at)].set(low)
    longest = extent.index(max(extent))
    index_at[longest] = (index_at[longest] + 1) % extent[longest]
    return entries.at[tuple(index_at)].set(largest)


def level_of(key, dims, cuts, smallest, top_value):
    loudness, own = 1.0, jax.random.fold_in(key, 6)
    for axis_at, shards_of in cuts:
        heights = jnp.exp(jax.random.uniform(jax.random.fold_in(own, axis_at), (shards_of,), jnp.float32, smallest / len(cuts), top_value / len(cuts)))
        loudness = loudness * jnp.repeat(heights, dims[axis_at] // shards_of).reshape([-1 if axis == axis_at else 1 for axis in range(len(dims))])
    return loudness


def shared_out(key, own, number, rows, amount, top, limit, slope):
    sequence = jax.random.permutation(key, amount)
    heavy_load, ordinary = portions_of(amount, rows * top, limit, slope, True), portions_of(amount, rows * top, limit, slope, False)
    places = jnp.arange(amount)

    def named(sizes, turn):
        used = int((sizes > 0).sum())
        fixed = max(1, used // 4)
        moved = fixed + (places - fixed + turn * (used - fixed)) % max(1, amount - fixed)
        return jnp.zeros((amount,), jnp.int32).at[sequence[jnp.where(places < fixed, places, moved)]].set(jnp.asarray(sizes, jnp.int32))

    sizes = jnp.where(number % 4 == 0, named(heavy_load, number // 4), named(ordinary, number - number // 4 - 1))
    mixed = jax.random.permutation(jax.random.fold_in(own, 3), amount)
    source_of, taker = mixed[0:amount // 2 * 2:2], mixed[1:amount // 2 * 2:2]
    slack = jnp.minimum(sizes[source_of] - 1, limit - sizes[taker]) // 2
    slack = jnp.where((source_of == sequence[0]) | (taker == sequence[0]) | (sizes[taker] == 0), 0, jnp.maximum(slack, 0))
    moved = jax.random.randint(jax.random.fold_in(own, 4), (amount // 2,), 0, 1 << 20) % (slack + 1)
    sizes = sizes.at[source_of].add(-moved).at[taker].add(moved)
    labels = jnp.searchsorted(jnp.cumsum(sizes), jnp.arange(rows * top), side="right").astype(jnp.int32)
    grid = labels.reshape(top, rows).T
    grid = grid[jax.random.permutation(jax.random.fold_in(own, 1), rows)]
    turn = jax.random.randint(jax.random.fold_in(own, 2), (rows, 1), 0, top)
    return jnp.take_along_axis(grid, (jnp.arange(top)[None, :] + turn) % top, axis=1)


def portions_of(amount, total, reach, lean, full):
    loads = [(1 << 20) // math.isqrt(rank ** lean) + 1 for rank in range(1, amount + 1)]
    largest = reach if full else min(reach, max(-(-total // amount), total * loads[0] // sum(loads)))
    least = 1 if total - largest >= amount - 1 else 0
    given, surplus = [largest] + [least] * (amount - 1), total - largest - least * (amount - 1)
    while surplus > 0:
        candidates = [i for i in range(1, amount) if given[i] < largest] or [i for i in range(1, amount) if given[i] < reach]
        mass, remaining = sum([loads[i] for i in candidates]), surplus
        for i in candidates:
            addition = min(reach - given[i], max(1, remaining * loads[i] // mass), surplus)
            given[i] = given[i] + addition
            surplus = surplus - addition
    return np.array(given)


def noise(stream_key, extent, deviation, most, shards=(), dtype=jnp.bfloat16):
    loudness = level_of(stream_key, extent, shards, -0.22, 0.18) if shards else 1.0
    drawn = jax.random.normal(stream_key, extent, jnp.float32) * deviation * loudness
    return jnp.minimum(jnp.maximum(drawn, -most), most).astype(dtype)


def setup_inputs(seed: int = 0) -> dict:
    arg_keys = jax.random.split(jax.random.key(seed), 11)
    points = noise(arg_keys[0], (POINTS, C_PT), 1.0, 6.0, ((0, 128),))
    point_brick_keys = jax.random.split(jax.random.fold_in(arg_keys[1], 1), POINTS // P_DEV)
    point_brick_turns = jax.random.permutation(jax.random.fold_in(arg_keys[1], 3), POINTS // P_DEV)
    point_brick = jax.vmap(lambda own, number: shared_out(jax.random.fold_in(arg_keys[1], 2), own, number, P_DEV, DEVICES, 1, CAP, 2))(point_brick_keys, point_brick_turns).reshape((POINTS, 1))
    point_voxel = plant(jax.random.randint(arg_keys[2], (POINTS,), 0, V), jax.random.fold_in(arg_keys[2], 1), 0, V - 1).astype(jnp.int32)
    send_rows = plant(jax.random.randint(arg_keys[3], (TILES, LAYERS, 4, RIM), 0, V), jax.random.fold_in(arg_keys[3], 1), 0, V - 1).astype(jnp.int32)
    pair_in = draw_pair_in(jax.random.fold_in(arg_keys[10], 71), 0)
    pair_out = draw_pair_out(jax.random.fold_in(arg_keys[10], 71), 0)
    bev_cell = plant(jax.random.randint(arg_keys[6], (TILES, LAYERS, V), 0, BX * BY), jax.random.fold_in(arg_keys[6], 1), 0, (BX * BY) - 1).astype(jnp.int32)
    conv_weight = noise(arg_keys[7], (27, C_PT, C_OUT), (8 * C_PT) ** -0.5, 0.1875)
    head_weight = noise(arg_keys[8], (9, C_OUT, C_HEAD), (9 * C_OUT) ** -0.5, 0.125)
    head_cot = noise(arg_keys[9], (TILES * BX, BY, C_HEAD), (1.0 / (TILES * BX * BY) ** 0.5), 0.0234375, ((0, 16),))
    return {"points": points, "point_brick": point_brick, "point_voxel": point_voxel, "send_rows": send_rows, "pair_in": pair_in, "pair_out": pair_out, "bev_cell": bev_cell, "conv_weight": conv_weight, "head_weight": head_weight, "head_cot": head_cot}


def window_patches(padded, height_rows, width_cols, flipped):
    pieces = []
    for row_off in range(3):
        for col_off in range(3):
            first_row = 2 - row_off if flipped else row_off
            first_col = 2 - col_off if flipped else col_off
            pieces.append(padded[first_row:first_row + height_rows, first_col:first_col + width_cols])
    return jnp.concatenate(pieces, axis=-1)


def silu_slope(pre_act):
    sigma = jax.nn.sigmoid(pre_act)
    return sigma * (1.0 + pre_act * (1.0 - sigma))


def brick_forward(ext_table, pooled_own, pair_src, pair_dst, conv_weight):
    gathered = ext_table[pair_src]
    offset_terms = jnp.einsum("kpc,kco->kpo", gathered.astype(jnp.float32), conv_weight[:26].astype(jnp.float32))
    voxels = pooled_own.shape[0]
    summed = jax.ops.segment_sum(offset_terms.reshape(-1, offset_terms.shape[-1]), pair_dst.reshape(-1), num_segments=voxels + 1)[:voxels]
    centre = jnp.dot(pooled_own, conv_weight[26], preferred_element_type=jnp.float32)
    return gathered, summed + centre


def reference(points, point_brick, point_voxel, send_rows, pair_in, pair_out, bev_cell, conv_weight, head_weight, head_cot):
    brick_count = TILES * LAYERS
    voxel_ids = (point_brick[:, 0] * V + point_voxel).astype(jnp.int32)
    pooled = jax.ops.segment_sum(points.astype(jnp.float32), voxel_ids, num_segments=brick_count * V)
    pooled = pooled.astype(jnp.bfloat16).reshape(TILES, LAYERS, V, C_PT)
    picker = jax.vmap(jax.vmap(lambda source, chosen: source[chosen]))
    outgoing = [picker(pooled, send_rows[:, :, side]) for side in range(4)]
    from_left = jnp.concatenate([jnp.zeros_like(outgoing[1][:1]), outgoing[1][:-1]], axis=0)
    from_right = jnp.concatenate([outgoing[0][1:], jnp.zeros_like(outgoing[0][:1])], axis=0)
    from_below = jnp.concatenate([jnp.zeros_like(outgoing[3][:, :1]), outgoing[3][:, :-1]], axis=1)
    from_above = jnp.concatenate([outgoing[2][:, 1:], jnp.zeros_like(outgoing[2][:, :1])], axis=1)
    zero_row = jnp.zeros((TILES, LAYERS, 1, C_PT), jnp.bfloat16)
    tables = jnp.concatenate([pooled, from_left, from_right, from_below, from_above, zero_row], axis=2)
    tables = tables.reshape(brick_count, V + 4 * RIM + 1, C_PT)
    pooled_flat = pooled.reshape(brick_count, V, C_PT)
    src_flat = pair_in.reshape(brick_count, 26, PAIRS)
    dst_flat = pair_out.reshape(brick_count, 26, PAIRS)
    cell_flat = bev_cell.reshape(brick_count, V)

    def collapse(brick_items):
        ext_table, pooled_own, pair_src, pair_dst, bev_cells = brick_items
        unused, pre_act = brick_forward(ext_table, pooled_own, pair_src, pair_dst, conv_weight)
        activated = jax.nn.silu(pre_act).astype(jnp.bfloat16)
        return jax.ops.segment_sum(activated.astype(jnp.float32), bev_cells, num_segments=BX * BY)

    columns = lax.map(collapse, (tables, pooled_flat, src_flat, dst_flat, cell_flat))
    bev_grid = jnp.sum(columns.reshape(TILES, LAYERS, BX * BY, C_OUT), axis=1)
    bev_grid = bev_grid.astype(jnp.bfloat16).reshape(TILES * BX, BY, C_OUT)
    bev_pad = jnp.pad(bev_grid, ((1, 1), (1, 1), (0, 0)))
    patches = window_patches(bev_pad, TILES * BX, BY, False).reshape(-1, 9 * C_OUT)
    head_out = jnp.dot(patches, head_weight.reshape(9 * C_OUT, C_HEAD), preferred_element_type=jnp.float32)
    head_out = head_out.astype(jnp.bfloat16).reshape(TILES * BX, BY, C_HEAD)
    cot_flat = head_cot.reshape(-1, C_HEAD)
    head_grad = lax.dot_general(patches, cot_flat, (((0,), (0,)), ((), ())), preferred_element_type=jnp.float32)
    head_grad = head_grad.reshape(9, C_OUT, C_HEAD)
    cot_pad = jnp.pad(head_cot, ((1, 1), (1, 1), (0, 0)))
    flipped = window_patches(cot_pad, TILES * BX, BY, True).reshape(-1, 9 * C_HEAD)
    back_weight = jnp.transpose(head_weight, (0, 2, 1)).reshape(9 * C_HEAD, C_OUT)
    bev_grad = jnp.dot(flipped, back_weight, preferred_element_type=jnp.float32).astype(jnp.bfloat16)
    bev_grad = bev_grad.reshape(TILES, BX * BY, C_OUT)
    tile_of = (jnp.arange(brick_count) // LAYERS).astype(jnp.int32)

    def accumulate(running, brick_items):
        ext_table, pooled_own, pair_src, pair_dst, bev_cells, tile_index = brick_items
        gathered, pre_act = brick_forward(ext_table, pooled_own, pair_src, pair_dst, conv_weight)
        upstream = bev_grad[tile_index][bev_cells]
        pre_grad = (upstream.astype(jnp.float32) * silu_slope(pre_act)).astype(jnp.bfloat16)
        padded_grad = jnp.concatenate([pre_grad, jnp.zeros((1, C_OUT), jnp.bfloat16)], axis=0)
        dst_grad = padded_grad[pair_dst]
        off_grad = jnp.einsum("kpc,kpo->kco", gathered.astype(jnp.float32), dst_grad.astype(jnp.float32))
        centre_grad = lax.dot_general(pooled_own, pre_grad, (((0,), (0,)), ((), ())), preferred_element_type=jnp.float32)
        return running + jnp.concatenate([off_grad, centre_grad[None]], axis=0), None

    conv_grad, unused = lax.scan(accumulate, jnp.zeros((27, C_PT, C_OUT), jnp.float32), (tables, pooled_flat, src_flat, dst_flat, cell_flat, tile_of))
    return head_out, conv_grad, head_grad
```

```python
import functools

import jax
import jax.numpy as jnp
from jax import lax
from jax.experimental import pallas as pl
from jax.experimental.pallas import tpu as pltpu
from jax.sharding import Mesh, PartitionSpec as P

BF = jnp.bfloat16
F32 = jnp.float32
I32 = jnp.int32
PLANE = ("x", "z")
HEIGHT = ("y", "c")
ALL = ("x", "z", "y", "c")
CAP = 32
ROWS = 40
OFFS = 26
VMEM = pl.BlockSpec(memory_space=pltpu.VMEM)
SMEM = pl.BlockSpec(memory_space=pltpu.SMEM)


def iota(shape, axis):
    return lax.broadcasted_iota(I32, shape, axis)


def hot(mask):
    return jnp.where(mask, 1.0, 0.0).astype(BF)


def dot(a, b):
    return jnp.dot(a, b, preferred_element_type=F32)


def dot_rows(a, b):
    return lax.dot_general(a, b, (((0,), (0,)), ((), ())), preferred_element_type=F32)


def dot_lanes(a, b):
    return lax.dot_general(a, b, (((1,), (1,)), ((), ())), preferred_element_type=F32)


def call(kernel, outs, args, specs=None, scratch=(), flops=0, limit=56):
    return pl.pallas_call(
        kernel,
        out_shape=outs,
        in_specs=[VMEM] * len(args) if specs is None else specs,
        out_specs=jax.tree.map(lambda _: VMEM, outs),
        scratch_shapes=list(scratch),
        compiler_params=pltpu.CompilerParams(vmem_limit_bytes=limit * 1024 * 1024),
        cost_estimate=pl.CostEstimate(flops=flops, bytes_accessed=4 << 20, transcendentals=0),
    )(*args)


def fill_kernel(brick_ref, voxel_ref, points_ref, out_ref, slot_ref):
    step = 256
    total = brick_ref.shape[1]
    upper = hot(iota((step, step), 0) <= iota((step, step), 1))
    run = jnp.zeros((128, 1), F32)
    high = jnp.zeros((128, 128), F32)
    low = jnp.zeros((128, 128), F32)
    for first in range(0, total, step):
        brick = brick_ref[:, first : first + step]
        voxel = voxel_ref[:, first : first + step]
        member = jnp.where(brick == iota((128, step), 0), 1.0, 0.0)
        counts = dot(member.astype(BF), upper) + run
        rank = (jnp.sum(member * counts, axis=0, keepdims=True) - 1.0).astype(I32)
        run = counts[:, step - 1 :]
        slot_ref[:, first : first + step] = brick * CAP + rank
        ranks = hot(rank == (iota((128, step), 0) & (CAP - 1)))
        top = (voxel >> 5).astype(F32)
        bottom = (voxel & 31).astype(F32)
        high = high + dot_lanes((member * top).astype(BF), ranks)
        low = low + dot_lanes((member * bottom).astype(BF), ranks)
    place = iota((128, ROWS - CAP, 128), 1)
    codes = jnp.where(place == 0, high[:, None, :], jnp.where(place == 1, low[:, None, :], 0.0))
    out_ref[:, CAP:ROWS, :] = codes.astype(BF)

    def step_fill(i, carry):
        wanted = iota((256, total), 0) + i * 256
        rows = dot(hot(slot_ref[...] == wanted), points_ref[...]).astype(BF)
        out_ref[pl.ds(i * 8, 8), 0:CAP, :] = rows.reshape(8, CAP, 128)
        return carry

    lax.fori_loop(0, 16, step_fill, 0)


def pool_kernel(got_ref, rim_ref, pooled_ref, rows_ref, acc_ref):
    voxels = pooled_ref.shape[0]

    def step_pool(i, carry):
        codes = got_ref[pl.ds(i * 8, 8), CAP:ROWS, :].astype(F32)
        ids = codes[:, 0, :] * 32.0 + codes[:, 1, :]
        wide = jnp.concatenate([ids, ids], axis=1)
        own = (iota((8, 256), 1) >> 5) == iota((8, 256), 0)
        row = jnp.sum(jnp.where(own, wide, 0.0), axis=0, keepdims=True).astype(I32)
        match = hot(row == iota((voxels, 256), 0))
        part = dot(match, got_ref[pl.ds(i * 8, 8), 0:CAP, :].reshape(256, 128))
        acc_ref[...] = jnp.where(i == 0, part, acc_ref[...] + part)
        return carry

    acc_ref[...] = jnp.zeros_like(acc_ref)
    lax.fori_loop(0, 16, step_pool, 0)
    pooled = acc_ref[...].astype(BF)
    pooled_ref[...] = pooled
    rows_ref[...] = dot(hot(rim_ref[...] == iota((256, voxels), 1)), pooled).astype(BF)


def gather_kernel(pooled_ref, src_ref, out_ref):
    voxels = pooled_ref.shape[0]
    for k in range(OFFS):
        match = hot(src_ref[:, k : k + 1] == iota((256, voxels), 1))
        out_ref[k * 256 : (k + 1) * 256, :] = dot(match, pooled_ref[...]).astype(BF)


def conv_kernel(
    core_ref,
    pooled_ref,
    picked_ref,
    left_ref,
    right_ref,
    below_ref,
    above_ref,
    src_ref,
    dst_ref,
    weight_ref,
    upstream_ref,
    window_ref,
    act_ref,
    keep_ref,
    send_ref,
    table_ref,
    pre_ref,
    grad_ref,
):
    voxels = pooled_ref.shape[0]
    rim = jnp.concatenate(
        [left_ref[...], right_ref[...], below_ref[...], above_ref[...]], axis=0
    )
    for k in range(OFFS):
        match = hot(src_ref[:, k : k + 1] == iota((256, 256), 1) + voxels)
        rows = picked_ref[k * 256 : (k + 1) * 256, :].astype(F32) + dot(match, rim)
        place = hot(dst_ref[k : k + 1, :] == iota((voxels, 256), 0))
        table_ref[:, k * 128 : (k + 1) * 128] = dot(place, rows.astype(BF)).astype(BF)
    table_ref[:, OFFS * 128 :] = pooled_ref[...]
    for m in range(0, voxels, 256):
        pre = dot(table_ref[m : m + 256, :], weight_ref[...])
        sigma = 1.0 / (1.0 + jnp.exp(-pre))
        act_ref[m : m + 256, :] = (pre * sigma).astype(BF)
        slope = sigma * (1.0 + pre * (1.0 - sigma))
        grad_ref[m : m + 256, :] = (upstream_ref[m : m + 256, :].astype(F32) * slope).astype(BF)
    first = core_ref[0] == 0
    for k in range(OFFS + 1):
        full = dot_rows(table_ref[:, k * 128 : (k + 1) * 128], grad_ref[...]).astype(F32)
        lo, hi = full[:, :128], full[:, 128:]
        keep_ref[k * 128 : (k + 1) * 128, :] = jnp.where(first, lo, hi).astype(BF)
        send_ref[k * 128 : (k + 1) * 128, :] = jnp.where(first, hi, lo).astype(BF)
    base = (OFFS + 1) * 128
    for k in range(9):
        full = dot_rows(act_ref[...], window_ref[:, k * 128 : (k + 1) * 128])
        lo, hi = full[:128], full[128:]
        at = base + k * 128
        keep_ref[at : at + 128, :] = jnp.where(first, lo, hi).astype(BF)
        send_ref[at : at + 128, :] = jnp.where(first, hi, lo).astype(BF)


def column_kernel(core_ref, cell_ref, act_ref, keep_ref, send_ref):
    core = core_ref[0]

    def step_column(i, carry):
        y, part = i // 2, i % 2
        for out_ref, which in ((keep_ref, core), (send_ref, 1 - core)):
            start = (y * 2 + which) * 512 + part * 256
            match = hot(cell_ref[...] == iota((256, cell_ref.shape[1]), 0) + start)
            out_ref[pl.ds(i * 256, 256), :] = dot(match, act_ref[...]).astype(BF)
        return carry

    lax.fori_loop(0, 8, step_column, 0)


def shifts(rows):
    total = rows.shape[0]
    y = iota(rows.shape, 0) & 63
    wide = rows.astype(F32)
    lower = jnp.where(y == 0, 0.0, pltpu.roll(wide, 1, 0))
    upper = jnp.where(y == 63, 0.0, pltpu.roll(wide, total - 1, 0))
    return [lower.astype(BF), rows, upper.astype(BF)]


def window_kernel(low_ref, cot_ref, high_ref, cell_ref, back_ref, window_ref, up_ref, moved_ref, patch_ref):
    cells = cot_ref.shape[0]
    for at, ref in ((0, low_ref), (64, cot_ref), (64 + cells, high_ref)):
        size = ref.shape[0]
        block = min(size, 512)
        for m in range(0, size, block):
            for b, moved in enumerate(shifts(ref[m : m + block, :])):
                moved_ref[b, at + m : at + m + block, :] = moved
    for a in range(3):
        for b in range(3):
            k = 3 * a + b
            patch_ref[:, k * 128 : (k + 1) * 128] = moved_ref[2 - b, (2 - a) * 64 : (2 - a) * 64 + cells, :]

    def step_window(i, carry):
        match = hot(cell_ref[pl.ds(i * 256, 256), :] == iota((256, cells), 1))
        for first in (0, 256, 512, 768, 1024):
            last = min(first + 256, 1152)
            window_ref[pl.ds(i * 256, 256), first:last] = dot(match, patch_ref[:, first:last]).astype(BF)
        up_ref[pl.ds(i * 256, 256), :] = dot(window_ref[pl.ds(i * 256, 256), :], back_ref[...]).astype(BF)
        return carry

    lax.fori_loop(0, 4, step_window, 0)


def head_kernel(low_ref, own_ref, high_ref, weight_ref, out_ref, moved_ref):
    size = own_ref.shape[0]
    for at, ref in ((0, low_ref), (64, own_ref), (64 + size, high_ref)):
        for b, moved in enumerate(shifts(ref[...])):
            moved_ref[b, at : at + ref.shape[0], :] = moved
    total = jnp.zeros(out_ref.shape, F32)
    for a in range(3):
        for b in range(3):
            total = total + dot(moved_ref[b, a * 64 : a * 64 + size, :], weight_ref[3 * a + b])
    out_ref[...] = total.astype(BF)


def chain(block, axes, by):
    count = lax.axis_size(axes)
    return lax.ppermute(
        block, axes, [(i, i + by) for i in range(count) if 0 <= i + by < count]
    )


def swap(block):
    return lax.ppermute(block, "c", [(0, 1), (1, 0)])


def exchange(block, axes):
    return lax.all_to_all(block, axes, split_axis=0, concat_axis=0, tiled=True)


def local(
    points,
    point_brick,
    point_voxel,
    send_rows,
    pair_in,
    pair_out,
    bev_cell,
    conv_weight,
    head_weight,
    head_cot,
):
    shape = jax.ShapeDtypeStruct
    voxels = bev_cell.shape[2]
    total = points.shape[0]
    core = lax.axis_index("c").astype(I32).reshape(1)

    ready = call(
        fill_kernel,
        shape((128, ROWS, 128), BF),
        (point_brick.reshape(1, total), point_voxel.reshape(1, total), points),
        scratch=[pltpu.VMEM((1, total), I32)],
        flops=3 << 30,
    )
    got = exchange(ready, ALL)

    cot = head_cot.reshape(-1, 128)
    cells = cot.shape[0]
    cot_low = chain(cot[cells - 64 :], PLANE, 1)
    cot_high = chain(cot[:64], PLANE, -1)
    back_weight = jnp.transpose(head_weight, (0, 2, 1)).reshape(9 * 128, 256)
    window, upstream = call(
        window_kernel,
        [shape((voxels, 9 * 128), BF), shape((voxels, 256), BF)],
        (cot_low, cot, cot_high, bev_cell.reshape(voxels, 1), back_weight),
        scratch=[pltpu.VMEM((3, cells + 128, 128), BF), pltpu.VMEM((cells, 9 * 128), BF)],
        flops=10 << 30,
    )

    pooled, outgoing = call(
        pool_kernel,
        [shape((voxels, 128), BF), shape((256, 128), BF)],
        (got, send_rows.reshape(256, 1)),
        scratch=[pltpu.VMEM((voxels, 128), F32)],
        flops=2 << 30,
    )
    from_left = chain(outgoing[64:128], PLANE, 1)
    from_right = chain(outgoing[0:64], PLANE, -1)
    from_below = chain(outgoing[192:256], HEIGHT, 1)
    from_above = chain(outgoing[128:192], HEIGHT, -1)
    sources = jnp.transpose(pair_in[0, 0])
    picked = call(
        gather_kernel, shape((OFFS * 256, 128), BF), (pooled, sources), flops=3 << 30
    )
    table_width = (OFFS + 1) * 128
    grad_rows = table_width + 9 * 128
    act, keep, send = call(
        conv_kernel,
        [shape((voxels, 256), BF), shape((grad_rows, 128), BF), shape((grad_rows, 128), BF)],
        (
            core,
            pooled,
            picked,
            from_left,
            from_right,
            from_below,
            from_above,
            sources,
            pair_out[0, 0],
            conv_weight.reshape(table_width, 256),
            upstream,
            window,
        ),
        specs=[SMEM] + [VMEM] * 11,
        scratch=[
            pltpu.VMEM((voxels, table_width), BF),
            pltpu.VMEM((8, 128), F32),
            pltpu.VMEM((voxels, 256), BF),
        ],
        flops=8 << 30,
    )

    both = (keep.astype(F32) + swap(send).astype(F32)).astype(BF)
    shares = exchange(both.reshape(64, grad_rows // 64, 128), ("x", "z", "y"))
    share = jnp.sum(shares.astype(F32), axis=0).astype(BF)
    mine = exchange(
        jnp.broadcast_to(share[None], (64,) + share.shape), ("x", "z", "y")
    ).reshape(36, 128, 128)

    column_keep, column_send = call(
        column_kernel,
        [shape((2048, 256), BF), shape((2048, 256), BF)],
        (core, bev_cell.reshape(1, voxels), act),
        specs=[SMEM, VMEM, VMEM],
        flops=3 << 30,
    )
    column = (column_keep.astype(F32) + swap(column_send).astype(F32)).astype(BF)
    column = exchange(column.reshape(4, 512, 256), "y")
    bev = jnp.sum(column.astype(F32), axis=0).astype(BF)
    bev_low = chain(bev[448:], ALL, 1)
    bev_high = chain(bev[:64], ALL, -1)
    head_out = call(
        head_kernel,
        shape((512, 128), BF),
        (bev_low, bev, bev_high, head_weight),
        scratch=[pltpu.VMEM((3, 640, 256), BF)],
        flops=1 << 30,
    )

    theirs = swap(mine)
    first = core[0] == 0
    lo = jnp.where(first, mine, theirs).astype(F32)
    hi = jnp.where(first, theirs, mine).astype(F32)
    conv_grad = jnp.concatenate([lo[:27], hi[:27]], axis=2)
    head_grad = jnp.concatenate([lo[27:], hi[27:]], axis=1)
    return (head_out.reshape(8, 64, 128), conv_grad, head_grad)


def solution(mesh):
    grid = Mesh(mesh.devices.reshape(4, 4, 4, 2), ALL)
    in_specs = (
        P(ALL, None),
        P(ALL, None),
        P(ALL),
        P(PLANE, HEIGHT, None, None),
        P(PLANE, HEIGHT, None, None),
        P(PLANE, HEIGHT, None, None),
        P(PLANE, HEIGHT, None),
        P(),
        P(),
        P(PLANE, None, None),
    )
    out_specs = (P(ALL, None, None), P(), P())
    return jax.shard_map(local, mesh=grid, in_specs=in_specs, out_specs=out_specs, check_vma=False)
```

```python
import functools

import jax
import jax.numpy as jnp
from jax import lax
from jax.experimental import pallas as pl
from jax.experimental.pallas import tpu as pltpu
from jax.sharding import Mesh, PartitionSpec as P

BF = jnp.bfloat16
F32 = jnp.float32
I32 = jnp.int32
PLANE = ("x", "z")
HEIGHT = ("y", "c")
ALL = ("x", "z", "y", "c")
CAP = 32
ROWS = 40
OFFS = 26
VMEM = pl.BlockSpec(memory_space=pltpu.VMEM)
SMEM = pl.BlockSpec(memory_space=pltpu.SMEM)


def iota(shape, axis):
    return lax.broadcasted_iota(I32, shape, axis)


def hot(mask):
    return jnp.where(mask, 1.0, 0.0).astype(BF)


def dot(a, b):
    return jnp.dot(a, b, preferred_element_type=F32)


def dot_rows(a, b):
    return lax.dot_general(a, b, (((0,), (0,)), ((), ())), preferred_element_type=F32)


def dot_lanes(a, b):
    return lax.dot_general(a, b, (((1,), (1,)), ((), ())), preferred_element_type=F32)


def call(kernel, outs, args, specs=None, scratch=(), flops=0, limit=56):
    return pl.pallas_call(
        kernel,
        out_shape=outs,
        in_specs=[VMEM] * len(args) if specs is None else specs,
        out_specs=jax.tree.map(lambda _: VMEM, outs),
        scratch_shapes=list(scratch),
        compiler_params=pltpu.CompilerParams(vmem_limit_bytes=limit * 1024 * 1024),
        cost_estimate=pl.CostEstimate(flops=flops, bytes_accessed=4 << 20, transcendentals=0),
    )(*args)


def fill_kernel(brick_ref, voxel_ref, points_ref, out_ref, slot_ref):
    step = 256
    total = brick_ref.shape[1]
    upper = hot(iota((step, step), 0) <= iota((step, step), 1))
    spans = [slice(first, first + step) for first in range(0, total, step)]
    masks = [brick_ref[:, span] == iota((128, step), 0) for span in spans]
    counts = dot(jnp.concatenate([hot(mask) for mask in masks], axis=0), upper)
    before = jnp.zeros((128, 1), F32)
    ranks = []
    for i, span in enumerate(spans):
        count = counts[i * 128 : (i + 1) * 128]
        rank = jnp.sum(jnp.where(masks[i], count + (before - 1.0), 0.0), axis=0, keepdims=True)
        before = before + count[:, step - 1 :]
        slot_ref[:, span] = brick_ref[:, span] * CAP + rank.astype(I32)
        ranks.append(rank.astype(I32))
    rank = jnp.concatenate(ranks, axis=1)
    member = brick_ref[...] == iota((128, total), 0)
    voxel = voxel_ref[...]
    high = jnp.where(member, (voxel >> 5).astype(F32), 0.0).astype(BF)
    low = jnp.where(member, (voxel & 31).astype(F32), 0.0).astype(BF)
    by_rank = hot(rank == (iota((128, total), 0) & (CAP - 1)))
    codes = dot_lanes(jnp.concatenate([high, low], axis=0), by_rank)
    place = iota((128, ROWS - CAP, 128), 1)
    rows = jnp.where(place == 0, codes[:128][:, None, :], 0.0)
    rows = jnp.where(place == 1, codes[128:][:, None, :], rows)
    out_ref[:, CAP:ROWS, :] = rows.astype(BF)
    for m in range(0, 128 * CAP, 512):
        match = hot(slot_ref[...] == iota((512, total), 0) + m)
        rows = dot(match, points_ref[...]).astype(BF)
        out_ref[m // CAP : (m + 512) // CAP, 0:CAP, :] = rows.reshape(512 // CAP, CAP, 128)


def pool_kernel(got_ref, rim_ref, pooled_ref, rows_ref, acc_ref):
    voxels = pooled_ref.shape[0]
    own = (iota((8, 256), 1) >> 5) == iota((8, 256), 0)
    for i in range(16):
        codes = got_ref[i * 8 : i * 8 + 8, CAP:ROWS, :].astype(F32)
        ids = codes[:, 0, :] * 32.0 + codes[:, 1, :]
        wide = jnp.concatenate([ids, ids], axis=1)
        row = jnp.sum(jnp.where(own, wide, 0.0), axis=0, keepdims=True).astype(I32)
        match = hot(row == iota((voxels, 256), 0))
        part = dot(match, got_ref[i * 8 : i * 8 + 8, 0:CAP, :].reshape(256, 128))
        acc_ref[...] = part if i == 0 else acc_ref[...] + part
    pooled = acc_ref[...].astype(BF)
    pooled_ref[...] = pooled
    rows_ref[...] = dot(hot(rim_ref[...] == iota((256, voxels), 1)), pooled).astype(BF)


def gather_kernel(pooled_ref, src_ref, out_ref, match_ref):
    voxels = pooled_ref.shape[0]
    for first in range(0, OFFS, 4):
        last = min(first + 4, OFFS)
        for k in range(first, last):
            match_ref[(k - first) * 256 : (k - first + 1) * 256, :] = hot(
                src_ref[:, k : k + 1] == iota((256, voxels), 1)
            )
        size = (last - first) * 256
        out_ref[first * 256 : last * 256, :] = dot(match_ref[:size, :], pooled_ref[...]).astype(BF)


def conv_kernel(
    core_ref,
    pooled_ref,
    picked_ref,
    left_ref,
    right_ref,
    below_ref,
    above_ref,
    src_ref,
    dst_ref,
    weight_ref,
    upstream_ref,
    window_ref,
    act_ref,
    keep_ref,
    send_ref,
    rows_ref,
    table_ref,
    grad_ref,
):
    voxels = pooled_ref.shape[0]
    rim = jnp.concatenate([left_ref[...], right_ref[...], below_ref[...], above_ref[...]], axis=0)
    for k in range(OFFS):
        match = hot(src_ref[:, k : k + 1] == iota((256, 256), 1) + voxels)
        rows = picked_ref[k * 256 : (k + 1) * 256, :].astype(F32) + dot(match, rim)
        rows_ref[k * 256 : (k + 1) * 256, :] = rows.astype(BF)
    for k in range(OFFS):
        place = hot(dst_ref[k : k + 1, :] == iota((voxels, 256), 0))
        table_ref[:, k * 128 : (k + 1) * 128] = dot(place, rows_ref[k * 256 : (k + 1) * 256, :]).astype(BF)
    table_ref[:, OFFS * 128 :] = pooled_ref[...]
    for m in range(0, voxels, 512):
        pre = dot(table_ref[m : m + 512, :], weight_ref[...])
        sigma = 1.0 / (1.0 + jnp.exp(-pre))
        act_ref[m : m + 512, :] = (pre * sigma).astype(BF)
        slope = sigma * (1.0 + pre * (1.0 - sigma))
        grad = upstream_ref[m : m + 512, :].astype(F32) * slope
        grad_ref[:, m : m + 512] = grad.T.astype(BF)
    first = core_ref[0] == 0
    wide = 9 * 128
    for n in range(0, (OFFS + 1) * 128, wide):
        full = dot(grad_ref[...], table_ref[:, n : n + wide])
        for at in range(0, wide, 128):
            lo, hi = full[:128, at : at + 128], full[128:, at : at + 128]
            keep_ref[n + at : n + at + 128, :] = jnp.where(first, lo, hi).T.astype(BF)
            send_ref[n + at : n + at + 128, :] = jnp.where(first, hi, lo).T.astype(BF)
    base = (OFFS + 1) * 128
    full = dot_rows(act_ref[...], window_ref[...])
    for at in range(0, wide, 128):
        lo, hi = full[:128, at : at + 128], full[128:, at : at + 128]
        keep_ref[base + at : base + at + 128, :] = jnp.where(first, lo, hi).astype(BF)
        send_ref[base + at : base + at + 128, :] = jnp.where(first, hi, lo).astype(BF)


def column_kernel(core_ref, cell_ref, act_ref, keep_ref, send_ref):
    core, here = core_ref[0], core_ref[1]
    for d in range(4):
        y = (here + d) & 3
        for out_ref, which in ((send_ref, 1 - core), (keep_ref, core)):
            for m in range(0, 512, 256):
                start = (y * 2 + which) * 512 + m
                match = hot(cell_ref[...] - start == iota((256, cell_ref.shape[1]), 0))
                out_ref[d * 512 + m : d * 512 + m + 256, :] = dot(match, act_ref[...]).astype(BF)


def shifts(rows):
    total = rows.shape[0]
    y = iota(rows.shape, 0) & 63
    wide = rows.astype(F32)
    lower = jnp.where(y == 0, 0.0, pltpu.roll(wide, 1, 0))
    upper = jnp.where(y == 63, 0.0, pltpu.roll(wide, total - 1, 0))
    return [lower.astype(BF), rows, upper.astype(BF)]


def window_kernel(cell_ref, low_ref, cot_ref, high_ref, weight_ref, window_ref, up_ref, pad_ref, rows_ref):
    voxels = window_ref.shape[0]
    pad_ref[:, 0:8, :] = jnp.zeros((66, 8, 128), F32)
    pad_ref[:, 72:80, :] = jnp.zeros((66, 8, 128), F32)
    pad_ref[0, 8:72, :] = low_ref[...].astype(F32)
    pad_ref[1:65, 8:72, :] = cot_ref[...].reshape(64, 64, 128).astype(F32)
    pad_ref[65, 8:72, :] = high_ref[...].astype(F32)

    def step_window(v, carry):
        cell = cell_ref[v]
        x = cell >> 6
        y = (cell & 63) + 7
        for a in range(3):
            rows_ref[a, pl.ds(v * 4, 4), :] = pad_ref[x + (2 - a), pl.ds(y, 4), :]
        return carry

    lax.fori_loop(0, voxels, step_window, 0, unroll=16)
    up = jnp.zeros(up_ref.shape, F32)
    for a in range(3):
        for b in range(3):
            k = 3 * a + b
            rows = rows_ref[a, pl.ds(2 - b, voxels, stride=4), :].astype(BF)
            window_ref[:, k * 128 : (k + 1) * 128] = rows
            up = up + dot_lanes(rows, weight_ref[k])
    up_ref[...] = up.astype(BF)


def final_kernel(mine_ref, theirs_ref, mine_head_ref, theirs_head_ref, core_ref, conv_ref, head_ref):
    first = core_ref[0] == 0
    mine, theirs = mine_ref[...].astype(F32), theirs_ref[...].astype(F32)
    conv_ref[:, :, 0:128] = jnp.where(first, mine, theirs)
    conv_ref[:, :, 128:256] = jnp.where(first, theirs, mine)
    mine, theirs = mine_head_ref[...].astype(F32), theirs_head_ref[...].astype(F32)
    head_ref[:, 0:128, :] = jnp.where(first, mine, theirs)
    head_ref[:, 128:256, :] = jnp.where(first, theirs, mine)


def join(mine, theirs, core):
    block = lambda i: (i, 0, 0)
    head = lambda i: (i + OFFS + 1, 0, 0)
    return pl.pallas_call(
        final_kernel,
        grid=(9,),
        out_shape=[
            jax.ShapeDtypeStruct((OFFS + 1, 128, 256), F32),
            jax.ShapeDtypeStruct((9, 256, 128), F32),
        ],
        in_specs=[
            pl.BlockSpec((3, 128, 128), block),
            pl.BlockSpec((3, 128, 128), block),
            pl.BlockSpec((1, 128, 128), head),
            pl.BlockSpec((1, 128, 128), head),
            SMEM,
        ],
        out_specs=[pl.BlockSpec((3, 128, 256), block), pl.BlockSpec((1, 256, 128), block)],
    )(mine, theirs, mine, theirs, core)


def head_kernel(low_ref, own_ref, high_ref, weight_ref, out_ref, moved_ref):
    size = own_ref.shape[0]
    for at, ref in ((0, low_ref), (64, own_ref), (64 + size, high_ref)):
        for b, moved in enumerate(shifts(ref[...])):
            moved_ref[b, at : at + ref.shape[0], :] = moved
    total = jnp.zeros(out_ref.shape, F32)
    for a in range(3):
        for b in range(3):
            total = total + dot(moved_ref[b, a * 64 : a * 64 + size, :], weight_ref[3 * a + b])
    out_ref[...] = total.astype(BF)


def chain(block, axes, by):
    count = lax.axis_size(axes)
    return lax.ppermute(
        block, axes, [(i, i + by) for i in range(count) if 0 <= i + by < count]
    )


def swap(block):
    return lax.ppermute(block, "c", [(0, 1), (1, 0)])


def exchange(block, axes):
    return lax.all_to_all(block, axes, split_axis=0, concat_axis=0, tiled=True)


def local(
    points,
    point_brick,
    point_voxel,
    send_rows,
    pair_in,
    pair_out,
    bev_cell,
    conv_weight,
    head_weight,
    head_cot,
):
    shape = jax.ShapeDtypeStruct
    voxels = bev_cell.shape[2]
    total = points.shape[0]
    core = jnp.stack([lax.axis_index("c"), lax.axis_index("y")]).astype(I32)

    ready = call(
        fill_kernel,
        shape((128, ROWS, 128), BF),
        (point_brick.reshape(1, total), point_voxel.reshape(1, total), points),
        scratch=[pltpu.VMEM((1, total), I32)],
        flops=3 << 30,
    )
    cot = head_cot.reshape(-1, 128)
    cells = cot.shape[0]
    cot_low = chain(cot[cells - 64 :], PLANE, 1)
    cot_high = chain(cot[:64], PLANE, -1)
    ready, cot_low, cot_high = lax.optimization_barrier((ready, cot_low, cot_high))
    got = exchange(ready, ALL)

    window, upstream = call(
        window_kernel,
        [shape((voxels, 9 * 128), BF), shape((voxels, 256), BF)],
        (bev_cell.reshape(voxels), cot_low, cot, cot_high, head_weight),
        specs=[SMEM] + [VMEM] * 4,
        scratch=[pltpu.VMEM((66, 80, 128), F32), pltpu.VMEM((3, 4 * voxels, 128), F32)],
        flops=1 << 30,
    )

    pooled, outgoing = call(
        pool_kernel,
        [shape((voxels, 128), BF), shape((256, 128), BF)],
        (got, send_rows.reshape(256, 1)),
        scratch=[pltpu.VMEM((voxels, 128), F32)],
        flops=2 << 30,
    )
    from_left = chain(outgoing[64:128], PLANE, 1)
    from_right = chain(outgoing[0:64], PLANE, -1)
    from_below = chain(outgoing[192:256], HEIGHT, 1)
    from_above = chain(outgoing[128:192], HEIGHT, -1)
    sources = jnp.transpose(pair_in[0, 0])
    picked = call(
        gather_kernel,
        shape((OFFS * 256, 128), BF),
        (pooled, sources),
        scratch=[pltpu.VMEM((1024, voxels), BF)],
        flops=3 << 30,
    )
    table_width = (OFFS + 1) * 128
    grad_rows = table_width + 9 * 128
    act, keep, send = call(
        conv_kernel,
        [shape((voxels, 256), BF), shape((grad_rows, 128), BF), shape((grad_rows, 128), BF)],
        (
            core,
            pooled,
            picked,
            from_left,
            from_right,
            from_below,
            from_above,
            sources,
            pair_out[0, 0],
            conv_weight.reshape(table_width, 256),
            upstream,
            window,
        ),
        specs=[SMEM] + [VMEM] * 11,
        scratch=[
            pltpu.VMEM((OFFS * 256, 128), BF),
            pltpu.VMEM((voxels, table_width), BF),
            pltpu.VMEM((256, voxels), BF),
        ],
        flops=8 << 30,
    )

    both = (keep.astype(F32) + swap(send).astype(F32)).astype(BF)
    both, act = lax.optimization_barrier((both, act))
    shares = exchange(both.reshape(64, grad_rows // 64, 128), ("x", "z", "y"))
    column_keep, column_send = call(
        column_kernel,
        [shape((2048, 256), BF), shape((2048, 256), BF)],
        (core, bev_cell.reshape(1, voxels), act),
        specs=[SMEM, VMEM, VMEM],
        flops=3 << 30,
    )
    column = (column_keep.astype(F32) + swap(column_send).astype(F32)).astype(BF)
    bev = column[:512].astype(F32)
    for d in (1, 2, 3):
        sent = column[d * 512 : (d + 1) * 512]
        bev = bev + lax.ppermute(sent, "y", [(i, (i + d) % 4) for i in range(4)]).astype(F32)
    bev = bev.astype(BF)
    share = jnp.sum(shares.astype(F32), axis=0).astype(BF)
    share, bev = lax.optimization_barrier((share, bev))
    mine = exchange(
        jnp.broadcast_to(share[None], (64,) + share.shape), ("x", "z", "y")
    ).reshape(36, 128, 128)
    bev_low = chain(bev[448:], ALL, 1)
    bev_high = chain(bev[:64], ALL, -1)
    head_out = call(
        head_kernel,
        shape((512, 128), BF),
        (bev_low, bev, bev_high, head_weight),
        scratch=[pltpu.VMEM((3, 640, 256), BF)],
        flops=1 << 30,
    )

    mine, head_out = lax.optimization_barrier((mine, head_out))
    conv_grad, head_grad = join(mine, swap(mine), core)
    return (head_out.reshape(8, 64, 128), conv_grad, head_grad)


def solution(mesh):
    grid = Mesh(mesh.devices.reshape(4, 4, 4, 2), ALL)
    in_specs = (
        P(ALL, None),
        P(ALL, None),
        P(ALL),
        P(PLANE, HEIGHT, None, None),
        P(PLANE, HEIGHT, None, None),
        P(PLANE, HEIGHT, None, None),
        P(PLANE, HEIGHT, None),
        P(),
        P(),
        P(PLANE, None, None),
    )
    out_specs = (P(ALL, None, None), P(), P())
    return jax.shard_map(local, mesh=grid, in_specs=in_specs, out_specs=out_specs, check_vma=False)
```

```python
import functools

import jax
import jax.numpy as jnp
from jax import lax
from jax.experimental import pallas as pl
from jax.experimental.pallas import tpu as pltpu
from jax.sharding import Mesh, PartitionSpec as P

BF = jnp.bfloat16
F32 = jnp.float32
I32 = jnp.int32
PLANE = ("x", "z")
HEIGHT = ("y", "c")
ALL = ("x", "z", "y", "c")
CAP = 32
ROWS = 40
OFFS = 26
VMEM = pl.BlockSpec(memory_space=pltpu.VMEM)
SMEM = pl.BlockSpec(memory_space=pltpu.SMEM)
ANY = pl.BlockSpec(memory_space=pl.ANY)


def iota(shape, axis):
    return lax.broadcasted_iota(I32, shape, axis)


def hot(mask):
    return jnp.where(mask, 1.0, 0.0).astype(BF)


def dot(a, b):
    return jnp.dot(a, b, preferred_element_type=F32)


def dot_rows(a, b):
    return lax.dot_general(a, b, (((0,), (0,)), ((), ())), preferred_element_type=F32)


def dot_lanes(a, b):
    return lax.dot_general(a, b, (((1,), (1,)), ((), ())), preferred_element_type=F32)


def call(kernel, outs, args, specs=None, scratch=(), flops=0, limit=56, out=VMEM):
    return pl.pallas_call(
        kernel,
        out_shape=outs,
        in_specs=[VMEM] * len(args) if specs is None else specs,
        out_specs=jax.tree.map(lambda _: out, outs),
        scratch_shapes=list(scratch),
        compiler_params=pltpu.CompilerParams(vmem_limit_bytes=limit * 1024 * 1024),
        cost_estimate=pl.CostEstimate(flops=flops, bytes_accessed=4 << 20, transcendentals=0),
    )(*args)


def fill_kernel(brick_ref, voxel_ref, points_ref, out_ref, slot_ref):
    step = 256
    total = brick_ref.shape[1]
    upper = hot(iota((step, step), 0) <= iota((step, step), 1))
    spans = [slice(first, first + step) for first in range(0, total, step)]
    masks = [brick_ref[:, span] == iota((128, step), 0) for span in spans]
    counts = dot(jnp.concatenate([hot(mask) for mask in masks], axis=0), upper)
    before = jnp.zeros((128, 1), F32)
    ranks = []
    for i, span in enumerate(spans):
        count = counts[i * 128 : (i + 1) * 128]
        rank = jnp.sum(jnp.where(masks[i], count + (before - 1.0), 0.0), axis=0, keepdims=True)
        before = before + count[:, step - 1 :]
        slot_ref[:, span] = brick_ref[:, span] * CAP + rank.astype(I32)
        ranks.append(rank.astype(I32))
    rank = jnp.concatenate(ranks, axis=1)
    member = brick_ref[...] == iota((128, total), 0)
    voxel = voxel_ref[...]
    high = jnp.where(member, (voxel >> 5).astype(F32), 0.0).astype(BF)
    low = jnp.where(member, (voxel & 31).astype(F32), 0.0).astype(BF)
    by_rank = hot(rank == (iota((128, total), 0) & (CAP - 1)))
    codes = dot_lanes(jnp.concatenate([high, low], axis=0), by_rank)
    place = iota((128, ROWS - CAP, 128), 1)
    rows = jnp.where(place == 0, codes[:128][:, None, :], 0.0)
    rows = jnp.where(place == 1, codes[128:][:, None, :], rows)
    out_ref[:, CAP:ROWS, :] = rows.astype(BF)
    for m in range(0, 128 * CAP, 512):
        match = hot(slot_ref[...] == iota((512, total), 0) + m)
        rows = dot(match, points_ref[...]).astype(BF)
        out_ref[m // CAP : (m + 512) // CAP, 0:CAP, :] = rows.reshape(512 // CAP, CAP, 128)


def pool_kernel(got_ref, rim_ref, pooled_ref, rows_ref, acc_ref):
    voxels = pooled_ref.shape[0]
    own = (iota((8, 256), 1) >> 5) == iota((8, 256), 0)
    for i in range(16):
        codes = got_ref[i * 8 : i * 8 + 8, CAP:ROWS, :].astype(F32)
        ids = codes[:, 0, :] * 32.0 + codes[:, 1, :]
        wide = jnp.concatenate([ids, ids], axis=1)
        row = jnp.sum(jnp.where(own, wide, 0.0), axis=0, keepdims=True).astype(I32)
        match = hot(row == iota((voxels, 256), 0))
        part = dot(match, got_ref[i * 8 : i * 8 + 8, 0:CAP, :].reshape(256, 128))
        acc_ref[...] = part if i == 0 else acc_ref[...] + part
    pooled = acc_ref[...].astype(BF)
    pooled_ref[...] = pooled
    rows_ref[...] = dot(hot(rim_ref[...] == iota((256, voxels), 1)), pooled).astype(BF)


def conv_kernel(
    core_ref,
    pooled_ref,
    left_ref,
    right_ref,
    swapped_ref,
    paired_ref,
    src_ref,
    dst_ref,
    weight_any,
    upstream_any,
    window_any,
    act_any,
    keep_any,
    send_any,
    wide_ref,
    rows_ref,
    table_ref,
    grad_ref,
    weight_ref,
    upstream_ref,
    window_ref,
    act_ref,
    keep_ref,
    send_ref,
    sems,
):
    voxels = pooled_ref.shape[0]
    loads = [
        pltpu.make_async_copy(weight_any, weight_ref, sems.at[0]),
        pltpu.make_async_copy(upstream_any, upstream_ref, sems.at[1]),
        pltpu.make_async_copy(window_any, window_ref, sems.at[2]),
    ]
    for load in loads:
        load.start()
    first = core_ref[0] == 0
    for g in range(4):
        wide_ref[:, g * 128 : (g + 1) * 128] = pooled_ref[g * 256 : (g + 1) * 256, :]
    swapped, paired = swapped_ref[...].astype(F32), paired_ref[...].astype(F32)
    wide_ref[0:64, 512:640] = left_ref[...]
    wide_ref[64:128, 512:640] = right_ref[...]
    wide_ref[128:192, 512:640] = jnp.where(first, paired, swapped).astype(BF)
    wide_ref[192:256, 512:640] = jnp.where(first, swapped, paired).astype(BF)
    row = src_ref[...] & 255
    group = src_ref[...] >> 8
    for k in range(OFFS):
        rows = dot(hot(row[:, k : k + 1] == iota((256, 256), 1)), wide_ref[...])
        side = jnp.broadcast_to(group[:, k : k + 1], (256, 128))
        picked = jnp.zeros((256, 128), F32)
        for g in range(5):
            picked = jnp.where(side == g, rows[:, g * 128 : (g + 1) * 128], picked)
        rows_ref[k * 256 : (k + 1) * 256, :] = picked.astype(BF)
    for k in range(OFFS):
        place = hot(dst_ref[k : k + 1, :] == iota((voxels, 256), 0))
        table_ref[:, k * 128 : (k + 1) * 128] = dot(place, rows_ref[k * 256 : (k + 1) * 256, :]).astype(BF)
    table_ref[:, OFFS * 128 :] = pooled_ref[...]
    loads[0].wait()
    loads[1].wait()
    for m in range(0, voxels, 512):
        pre = dot(table_ref[m : m + 512, :], weight_ref[...])
        sigma = 1.0 / (1.0 + jnp.exp(-pre))
        act_ref[m : m + 512, :] = (pre * sigma).astype(BF)
        slope = sigma * (1.0 + pre * (1.0 - sigma))
        grad = upstream_ref[m : m + 512, :].astype(F32) * slope
        grad_ref[:, m : m + 512] = grad.T.astype(BF)
    stores = [pltpu.make_async_copy(act_ref, act_any, sems.at[3])]
    stores[0].start()
    wide = 9 * 128
    for step in range(3):
        full = dot(grad_ref[...], table_ref[:, step * wide : (step + 1) * wide])
        for at in range(0, wide, 128):
            lo, hi = full[:128, at : at + 128], full[128:, at : at + 128]
            to = step * wide + at
            keep_ref[to : to + 128, :] = jnp.where(first, lo, hi).T.astype(BF)
            send_ref[to : to + 128, :] = jnp.where(first, hi, lo).T.astype(BF)
    loads[2].wait()
    base = (OFFS + 1) * 128
    stores += [
        pltpu.make_async_copy(send_ref.at[0:base], send_any.at[0:base], sems.at[4]),
        pltpu.make_async_copy(keep_ref.at[0:base], keep_any.at[0:base], sems.at[5]),
    ]
    stores[1].start()
    stores[2].start()
    full = dot_rows(act_ref[...], window_ref[...])
    for at in range(0, wide, 128):
        lo, hi = full[:128, at : at + 128], full[128:, at : at + 128]
        keep_ref[base + at : base + at + 128, :] = jnp.where(first, lo, hi).astype(BF)
        send_ref[base + at : base + at + 128, :] = jnp.where(first, hi, lo).astype(BF)
    stores += [
        pltpu.make_async_copy(send_ref.at[base : base + wide], send_any.at[base : base + wide], sems.at[6]),
        pltpu.make_async_copy(keep_ref.at[base : base + wide], keep_any.at[base : base + wide], sems.at[7]),
    ]
    stores[3].start()
    stores[4].start()
    for store in stores:
        store.wait()


def column_kernel(core_ref, cell_ref, act_ref, keep_ref, send_ref):
    core, here = core_ref[0], core_ref[1]
    for d in range(4):
        y = (here + d) & 3
        for out_ref, which in ((send_ref, 1 - core), (keep_ref, core)):
            for m in range(0, 512, 256):
                start = (y * 2 + which) * 512 + m
                match = hot(cell_ref[...] - start == iota((256, cell_ref.shape[1]), 0))
                out_ref[d * 512 + m : d * 512 + m + 256, :] = dot(match, act_ref[...]).astype(BF)


def shifts(rows):
    total = rows.shape[0]
    y = iota(rows.shape, 0) & 63
    wide = rows.astype(F32)
    lower = jnp.where(y == 0, 0.0, pltpu.roll(wide, 1, 0))
    upper = jnp.where(y == 63, 0.0, pltpu.roll(wide, total - 1, 0))
    return [lower.astype(BF), rows, upper.astype(BF)]


def window_kernel(cell_ref, low_ref, cot_ref, high_ref, weight_ref, window_ref, up_ref, pad_ref, rows_ref):
    voxels = window_ref.shape[0]
    pad_ref[:, 0:8, :] = jnp.zeros((66, 8, 128), F32)
    pad_ref[:, 72:80, :] = jnp.zeros((66, 8, 128), F32)
    pad_ref[0, 8:72, :] = low_ref[...].astype(F32)
    pad_ref[1:65, 8:72, :] = cot_ref[...].reshape(64, 64, 128).astype(F32)
    pad_ref[65, 8:72, :] = high_ref[...].astype(F32)

    def step_window(v, carry):
        cell = cell_ref[v]
        x = cell >> 6
        y = (cell & 63) + 7
        for a in range(3):
            rows_ref[a, pl.ds(v * 4, 4), :] = pad_ref[x + (2 - a), pl.ds(y, 4), :]
        return carry

    lax.fori_loop(0, voxels, step_window, 0, unroll=16)
    up = jnp.zeros(up_ref.shape, F32)
    for a in range(3):
        for b in range(3):
            k = 3 * a + b
            rows = rows_ref[a, pl.ds(2 - b, voxels, stride=4), :].astype(BF)
            window_ref[:, k * 128 : (k + 1) * 128] = rows
            up = up + dot_lanes(rows, weight_ref[k])
    up_ref[...] = up.astype(BF)


def final_kernel(mine_ref, theirs_ref, core_ref, conv_any, head_any, conv_ref, head_ref, sems):
    first = core_ref[0] == 0
    stores = []
    for i in range(9):
        for k in range(3 * i, 3 * i + 3):
            mine, theirs = mine_ref[k].astype(F32), theirs_ref[k].astype(F32)
            conv_ref[k, :, 0:128] = jnp.where(first, mine, theirs)
            conv_ref[k, :, 128:256] = jnp.where(first, theirs, mine)
        part = pl.ds(3 * i, 3)
        stores.append(pltpu.make_async_copy(conv_ref.at[part], conv_any.at[part], sems.at[2 * i]))
        stores[-1].start()
        mine, theirs = mine_ref[OFFS + 1 + i].astype(F32), theirs_ref[OFFS + 1 + i].astype(F32)
        head_ref[i, 0:128, :] = jnp.where(first, mine, theirs)
        head_ref[i, 128:256, :] = jnp.where(first, theirs, mine)
        stores.append(pltpu.make_async_copy(head_ref.at[i], head_any.at[i], sems.at[2 * i + 1]))
        stores[-1].start()
    for store in stores:
        store.wait()


def join(mine, theirs, core):
    conv, head = (OFFS + 1, 128, 256), (9, 256, 128)
    return pl.pallas_call(
        final_kernel,
        out_shape=[jax.ShapeDtypeStruct(conv, F32), jax.ShapeDtypeStruct(head, F32)],
        in_specs=[VMEM, VMEM, SMEM],
        out_specs=[ANY, ANY],
        scratch_shapes=[pltpu.VMEM(conv, F32), pltpu.VMEM(head, F32), pltpu.SemaphoreType.DMA((18,))],
        compiler_params=pltpu.CompilerParams(vmem_limit_bytes=32 * 1024 * 1024),
    )(mine, theirs, core)


def head_kernel(low_ref, own_ref, high_ref, weight_ref, out_ref, moved_ref):
    size = own_ref.shape[0]
    for at, ref in ((0, low_ref), (64, own_ref), (64 + size, high_ref)):
        for b, moved in enumerate(shifts(ref[...])):
            moved_ref[b, at : at + ref.shape[0], :] = moved
    total = jnp.zeros(out_ref.shape, F32)
    for a in range(3):
        for b in range(3):
            total = total + dot(moved_ref[b, a * 64 : a * 64 + size, :], weight_ref[3 * a + b])
    out_ref[...] = total.astype(BF)


def chain(block, axes, by):
    count = lax.axis_size(axes)
    return lax.ppermute(
        block, axes, [(i, i + by) for i in range(count) if 0 <= i + by < count]
    )


def swap(block):
    return lax.ppermute(block, "c", [(0, 1), (1, 0)])


def exchange(block, axes):
    return lax.all_to_all(block, axes, split_axis=0, concat_axis=0, tiled=True)


def local(
    points,
    point_brick,
    point_voxel,
    send_rows,
    pair_in,
    pair_out,
    bev_cell,
    conv_weight,
    head_weight,
    head_cot,
):
    shape = jax.ShapeDtypeStruct
    voxels = bev_cell.shape[2]
    total = points.shape[0]
    core = jnp.stack([lax.axis_index("c"), lax.axis_index("y")]).astype(I32)

    ready = call(
        fill_kernel,
        shape((128, ROWS, 128), BF),
        (point_brick.reshape(1, total), point_voxel.reshape(1, total), points),
        scratch=[pltpu.VMEM((1, total), I32)],
        flops=3 << 30,
    )
    cot = head_cot.reshape(-1, 128)
    cells = cot.shape[0]
    cot_low = chain(cot[cells - 64 :], PLANE, 1)
    cot_high = chain(cot[:64], PLANE, -1)
    ready, cot_low, cot_high = lax.optimization_barrier((ready, cot_low, cot_high))
    got = exchange(ready, ALL)

    window, upstream = call(
        window_kernel,
        [shape((voxels, 9 * 128), BF), shape((voxels, 256), BF)],
        (bev_cell.reshape(voxels), cot_low, cot, cot_high, head_weight),
        specs=[SMEM] + [VMEM] * 4,
        scratch=[pltpu.VMEM((66, 80, 128), F32), pltpu.VMEM((3, 4 * voxels, 128), F32)],
        flops=1 << 30,
    )

    sides = send_rows[0, 0]
    even = core[0] == 0
    sides = jnp.concatenate(
        [sides[:2], jnp.where(even, sides[3:], sides[2:3]), jnp.where(even, sides[2:3], sides[3:])]
    )
    pooled, outgoing = call(
        pool_kernel,
        [shape((voxels, 128), BF), shape((256, 128), BF)],
        (got, sides.reshape(256, 1)),
        scratch=[pltpu.VMEM((voxels, 128), F32)],
        flops=2 << 30,
    )
    layers = lax.axis_size(HEIGHT)
    pairs = [(i, i + 1) for i in range(1, layers - 1, 2)]
    from_left = chain(outgoing[64:128], PLANE, 1)
    from_right = chain(outgoing[0:64], PLANE, -1)
    paired = lax.ppermute(outgoing[192:256], HEIGHT, pairs + [(j, i) for i, j in pairs])
    swapped = swap(outgoing[128:192])
    table_width = (OFFS + 1) * 128
    grad_rows = table_width + 9 * 128
    act, keep, send = call(
        conv_kernel,
        [shape((voxels, 256), BF), shape((grad_rows, 128), BF), shape((grad_rows, 128), BF)],
        (
            core,
            pooled,
            from_left,
            from_right,
            swapped,
            paired,
            jnp.transpose(pair_in[0, 0]),
            pair_out[0, 0],
            conv_weight.reshape(table_width, 256),
            upstream,
            window,
        ),
        specs=[SMEM] + [VMEM] * 7 + [ANY] * 3,
        out=ANY,
        scratch=[
            pltpu.VMEM((256, 5 * 128), BF),
            pltpu.VMEM((OFFS * 256, 128), BF),
            pltpu.VMEM((voxels, table_width), BF),
            pltpu.VMEM((256, voxels), BF),
            pltpu.VMEM((table_width, 256), BF),
            pltpu.VMEM((voxels, 256), BF),
            pltpu.VMEM((voxels, 9 * 128), BF),
            pltpu.VMEM((voxels, 256), BF),
            pltpu.VMEM((grad_rows, 128), BF),
            pltpu.VMEM((grad_rows, 128), BF),
            pltpu.SemaphoreType.DMA((8,)),
        ],
        flops=8 << 30,
        limit=40,
    )

    arrived = swap(send)
    column_keep, column_send = call(
        column_kernel,
        [shape((2048, 256), BF), shape((2048, 256), BF)],
        (core, bev_cell.reshape(1, voxels), act),
        specs=[SMEM, VMEM, VMEM],
        flops=3 << 30,
    )
    arrived, column_keep, column_send = lax.optimization_barrier((arrived, column_keep, column_send))
    both = (keep.astype(F32) + arrived.astype(F32)).astype(BF)
    shares = exchange(both.reshape(64, grad_rows // 64, 128), ("x", "z", "y"))
    column = (column_keep.astype(F32) + swap(column_send).astype(F32)).astype(BF)
    ahead = [
        lax.ppermute(column[d * 512 : (d + 1) * 512], "y", [(i, (i + d) % 4) for i in range(4)])
        for d in (1, 2, 3)
    ]
    share = jnp.sum(shares.astype(F32), axis=0).astype(BF)
    bev = column[:512].astype(F32)
    for part in ahead:
        bev = bev + part.astype(F32)
    bev = bev.astype(BF)
    share, bev = lax.optimization_barrier((share, bev))
    mine = exchange(
        jnp.broadcast_to(share[None], (64,) + share.shape), ("x", "z", "y")
    ).reshape(36, 128, 128)
    bev_low = chain(bev[448:], ALL, 1)
    bev_high = chain(bev[:64], ALL, -1)
    head_out = call(
        head_kernel,
        shape((512, 128), BF),
        (bev_low, bev, bev_high, head_weight),
        scratch=[pltpu.VMEM((3, 640, 256), BF)],
        flops=1 << 30,
    )

    mine, head_out = lax.optimization_barrier((mine, head_out))
    conv_grad, head_grad = join(mine, swap(mine), core)
    return (head_out.reshape(8, 64, 128), conv_grad, head_grad)


def solution(mesh):
    grid = Mesh(mesh.devices.reshape(4, 4, 4, 2), ALL)
    in_specs = (
        P(ALL, None),
        P(ALL, None),
        P(ALL),
        P(PLANE, HEIGHT, None, None),
        P(PLANE, HEIGHT, None, None),
        P(PLANE, HEIGHT, None, None),
        P(PLANE, HEIGHT, None),
        P(),
        P(),
        P(PLANE, None, None),
    )
    out_specs = (P(ALL, None, None), P(), P())
    return jax.shard_map(local, mesh=grid, in_specs=in_specs, out_specs=out_specs, check_vma=False)
```

```python
import functools

import jax
import jax.numpy as jnp
from jax import lax
from jax.experimental import pallas as pl
from jax.experimental.pallas import tpu as pltpu
from jax.sharding import Mesh, PartitionSpec as P

BF = jnp.bfloat16
F32 = jnp.float32
I32 = jnp.int32
PLANE = ("x", "z")
HEIGHT = ("y", "c")
ALL = ("x", "z", "y", "c")
CAP = 32
ROWS = 40
OFFS = 26
EDGED = 576
VMEM = pl.BlockSpec(memory_space=pltpu.VMEM)
SMEM = pl.BlockSpec(memory_space=pltpu.SMEM)
ANY = pl.BlockSpec(memory_space=pl.ANY)


def iota(shape, axis):
    return lax.broadcasted_iota(I32, shape, axis)


def hot(mask):
    return jnp.where(mask, 1.0, 0.0).astype(BF)


def dot(a, b):
    return jnp.dot(a, b, preferred_element_type=F32)


def dot_rows(a, b):
    return lax.dot_general(a, b, (((0,), (0,)), ((), ())), preferred_element_type=F32)


def dot_lanes(a, b):
    return lax.dot_general(a, b, (((1,), (1,)), ((), ())), preferred_element_type=F32)


def call(kernel, outs, args, specs=None, scratch=(), flops=0, limit=56, out=VMEM):
    return pl.pallas_call(
        kernel,
        out_shape=outs,
        in_specs=[VMEM] * len(args) if specs is None else specs,
        out_specs=jax.tree.map(lambda _: out, outs),
        scratch_shapes=list(scratch),
        compiler_params=pltpu.CompilerParams(vmem_limit_bytes=limit * 1024 * 1024),
        cost_estimate=pl.CostEstimate(flops=flops, bytes_accessed=4 << 20, transcendentals=0),
    )(*args)


def fill_kernel(brick_ref, voxel_ref, points_ref, out_ref, slot_ref):
    step = 256
    total = brick_ref.shape[1]
    upper = hot(iota((step, step), 0) <= iota((step, step), 1))
    spans = [slice(first, first + step) for first in range(0, total, step)]
    masks = [brick_ref[:, span] == iota((128, step), 0) for span in spans]
    counts = dot(jnp.concatenate([hot(mask) for mask in masks], axis=0), upper)
    before = jnp.zeros((128, 1), F32)
    ranks = []
    for i, span in enumerate(spans):
        count = counts[i * 128 : (i + 1) * 128]
        rank = jnp.sum(jnp.where(masks[i], count + (before - 1.0), 0.0), axis=0, keepdims=True)
        before = before + count[:, step - 1 :]
        slot_ref[:, span] = brick_ref[:, span] * CAP + rank.astype(I32)
        ranks.append(rank.astype(I32))
    rank = jnp.concatenate(ranks, axis=1)
    member = brick_ref[...] == iota((128, total), 0)
    voxel = voxel_ref[...]
    high = jnp.where(member, (voxel >> 5).astype(F32), 0.0).astype(BF)
    low = jnp.where(member, (voxel & 31).astype(F32), 0.0).astype(BF)
    by_rank = hot(rank == (iota((128, total), 0) & (CAP - 1)))
    codes = dot_lanes(jnp.concatenate([high, low], axis=0), by_rank)
    place = iota((128, ROWS - CAP, 128), 1)
    rows = jnp.where(place == 0, codes[:128][:, None, :], 0.0)
    rows = jnp.where(place == 1, codes[128:][:, None, :], rows)
    out_ref[:, CAP:ROWS, :] = rows.astype(BF)
    for m in range(0, 128 * CAP, 512):
        match = hot(slot_ref[...] == iota((512, total), 0) + m)
        rows = dot(match, points_ref[...]).astype(BF)
        out_ref[m // CAP : (m + 512) // CAP, 0:CAP, :] = rows.reshape(512 // CAP, CAP, 128)


def pool_kernel(got_ref, rim_ref, pooled_ref, rows_ref, acc_ref):
    voxels = pooled_ref.shape[0]
    own = (iota((8, 256), 1) >> 5) == iota((8, 256), 0)
    for i in range(16):
        codes = got_ref[i * 8 : i * 8 + 8, CAP:ROWS, :].astype(F32)
        ids = codes[:, 0, :] * 32.0 + codes[:, 1, :]
        wide = jnp.concatenate([ids, ids], axis=1)
        row = jnp.sum(jnp.where(own, wide, 0.0), axis=0, keepdims=True).astype(I32)
        match = hot(row == iota((voxels, 256), 0))
        part = dot(match, got_ref[i * 8 : i * 8 + 8, 0:CAP, :].reshape(256, 128))
        acc_ref[...] = part if i == 0 else acc_ref[...] + part
    pooled = acc_ref[...].astype(BF)
    pooled_ref[...] = pooled
    rows_ref[...] = dot(hot(rim_ref[...] == iota((256, voxels), 1)), pooled).astype(BF)


def conv_kernel(
    core_ref,
    pooled_ref,
    left_ref,
    right_ref,
    swapped_ref,
    paired_ref,
    src_ref,
    dst_ref,
    weight_any,
    upstream_any,
    window_any,
    act_any,
    keep_any,
    send_any,
    wide_ref,
    rows_ref,
    table_ref,
    grad_ref,
    weight_ref,
    upstream_ref,
    window_ref,
    act_ref,
    keep_ref,
    send_ref,
    sems,
):
    voxels = pooled_ref.shape[0]
    loads = [
        pltpu.make_async_copy(weight_any, weight_ref, sems.at[0]),
        pltpu.make_async_copy(upstream_any, upstream_ref, sems.at[1]),
        pltpu.make_async_copy(window_any, window_ref, sems.at[2]),
    ]
    for load in loads:
        load.start()
    first = core_ref[0] == 0
    for g in range(4):
        wide_ref[:, g * 128 : (g + 1) * 128] = pooled_ref[g * 256 : (g + 1) * 256, :]
    swapped, paired = swapped_ref[...].astype(F32), paired_ref[...].astype(F32)
    wide_ref[0:64, 512:640] = left_ref[...]
    wide_ref[64:128, 512:640] = right_ref[...]
    wide_ref[128:192, 512:640] = jnp.where(first, paired, swapped).astype(BF)
    wide_ref[192:256, 512:640] = jnp.where(first, swapped, paired).astype(BF)
    row = src_ref[...] & 255
    group = src_ref[...] >> 8
    for k in range(OFFS):
        rows = dot(hot(row[:, k : k + 1] == iota((256, 256), 1)), wide_ref[...])
        side = jnp.broadcast_to(group[:, k : k + 1], (256, 128))
        picked = jnp.zeros((256, 128), F32)
        for g in range(5):
            picked = jnp.where(side == g, rows[:, g * 128 : (g + 1) * 128], picked)
        rows_ref[k * 256 : (k + 1) * 256, :] = picked.astype(BF)
    for k in range(OFFS):
        place = hot(dst_ref[k : k + 1, :] == iota((voxels, 256), 0))
        table_ref[:, k * 128 : (k + 1) * 128] = dot(place, rows_ref[k * 256 : (k + 1) * 256, :]).astype(BF)
    table_ref[:, OFFS * 128 :] = pooled_ref[...]
    loads[0].wait()
    loads[1].wait()
    for m in range(0, voxels, 512):
        pre = dot(table_ref[m : m + 512, :], weight_ref[...])
        sigma = 1.0 / (1.0 + jnp.exp(-pre))
        act_ref[m : m + 512, :] = (pre * sigma).astype(BF)
        slope = sigma * (1.0 + pre * (1.0 - sigma))
        grad = upstream_ref[m : m + 512, :].astype(F32) * slope
        grad_ref[:, m : m + 512] = grad.T.astype(BF)
    stores = [pltpu.make_async_copy(act_ref, act_any, sems.at[3])]
    stores[0].start()
    wide = 9 * 128
    for step in range(3):
        full = dot(grad_ref[...], table_ref[:, step * wide : (step + 1) * wide])
        for at in range(0, wide, 128):
            lo, hi = full[:128, at : at + 128], full[128:, at : at + 128]
            to = step * wide + at
            keep_ref[to : to + 128, :] = jnp.where(first, lo, hi).T.astype(BF)
            send_ref[to : to + 128, :] = jnp.where(first, hi, lo).T.astype(BF)
    loads[2].wait()
    base = (OFFS + 1) * 128
    stores += [
        pltpu.make_async_copy(send_ref.at[0:base], send_any.at[0:base], sems.at[4]),
        pltpu.make_async_copy(keep_ref.at[0:base], keep_any.at[0:base], sems.at[5]),
    ]
    stores[1].start()
    stores[2].start()
    full = dot_rows(act_ref[...], window_ref[...])
    for at in range(0, wide, 128):
        lo, hi = full[:128, at : at + 128], full[128:, at : at + 128]
        keep_ref[base + at : base + at + 128, :] = jnp.where(first, lo, hi).astype(BF)
        send_ref[base + at : base + at + 128, :] = jnp.where(first, hi, lo).astype(BF)
    stores += [
        pltpu.make_async_copy(send_ref.at[base : base + wide], send_any.at[base : base + wide], sems.at[6]),
        pltpu.make_async_copy(keep_ref.at[base : base + wide], keep_any.at[base : base + wide], sems.at[7]),
    ]
    stores[3].start()
    stores[4].start()
    for store in stores:
        store.wait()


def head_kernel(core_ref, cell_ref, act_ref, weight_ref, keep_ref, send_ref, wide_ref, total_ref):
    core, here = core_ref[0], core_ref[1]
    for a in range(3):
        for b in range(3):
            wide_ref[b, :, a * 128 : (a + 1) * 128] = weight_ref[3 * a + b]
    total_ref[...] = jnp.zeros_like(total_ref)
    y = iota((512, 256), 0) & 63
    for part in range(8):
        match = hot(cell_ref[...] - part * 512 == iota((512, cell_ref.shape[1]), 0))
        column = dot(match, act_ref[...])
        lower = jnp.where(y == 0, 0.0, pltpu.roll(column, 1, 0)).astype(BF)
        upper = jnp.where(y == 63, 0.0, pltpu.roll(column, 511, 0)).astype(BF)
        rows = dot(lower, wide_ref[0]) + dot(column.astype(BF), wide_ref[1]) + dot(upper, wide_ref[2])
        for a in range(3):
            at = (part * 8 + 2 - a) * 64
            total_ref[at : at + 512, :] += rows[:, a * 128 : (a + 1) * 128]
    for d in range(4):
        for out_ref, which in ((send_ref, 1 - core), (keep_ref, core)):
            layer = ((here + d) & 3) * 2 + which
            first = pl.multiple_of(layer * 512 + 64, 64)
            out_ref[d * EDGED : d * EDGED + 512, :] = total_ref[pl.ds(first, 512), :].astype(BF)
            beyond = jnp.where(layer == 7, total_ref[65 * 64 : 66 * 64, :], 0.0)
            beyond = jnp.where(layer == 0, total_ref[0:64, :], beyond)
            out_ref[d * EDGED + 512 : (d + 1) * EDGED, :] = beyond.astype(BF)


def window_kernel(cell_ref, low_ref, cot_ref, high_ref, weight_ref, window_ref, up_ref, pad_ref, rows_ref):
    voxels = window_ref.shape[0]
    pad_ref[:, 0:8, :] = jnp.zeros((66, 8, 128), F32)
    pad_ref[:, 72:80, :] = jnp.zeros((66, 8, 128), F32)
    pad_ref[0, 8:72, :] = low_ref[...].astype(F32)
    pad_ref[1:65, 8:72, :] = cot_ref[...].reshape(64, 64, 128).astype(F32)
    pad_ref[65, 8:72, :] = high_ref[...].astype(F32)

    def step_window(v, carry):
        cell = cell_ref[v]
        x = cell >> 6
        y = (cell & 63) + 7
        for a in range(3):
            rows_ref[a, pl.ds(v * 4, 4), :] = pad_ref[x + (2 - a), pl.ds(y, 4), :]
        return carry

    lax.fori_loop(0, voxels, step_window, 0, unroll=16)
    up = jnp.zeros(up_ref.shape, F32)
    for a in range(3):
        for b in range(3):
            k = 3 * a + b
            rows = rows_ref[a, pl.ds(2 - b, voxels, stride=4), :].astype(BF)
            window_ref[:, k * 128 : (k + 1) * 128] = rows
            up = up + dot_lanes(rows, weight_ref[k])
    up_ref[...] = up.astype(BF)


def final_kernel(mine_ref, theirs_ref, core_ref, conv_any, head_any, conv_ref, head_ref, sems):
    first = core_ref[0] == 0
    stores = []
    for i in range(9):
        for k in range(3 * i, 3 * i + 3):
            mine, theirs = mine_ref[k].astype(F32), theirs_ref[k].astype(F32)
            conv_ref[k, :, 0:128] = jnp.where(first, mine, theirs)
            conv_ref[k, :, 128:256] = jnp.where(first, theirs, mine)
        part = pl.ds(3 * i, 3)
        stores.append(pltpu.make_async_copy(conv_ref.at[part], conv_any.at[part], sems.at[2 * i]))
        stores[-1].start()
        mine, theirs = mine_ref[OFFS + 1 + i].astype(F32), theirs_ref[OFFS + 1 + i].astype(F32)
        head_ref[i, 0:128, :] = jnp.where(first, mine, theirs)
        head_ref[i, 128:256, :] = jnp.where(first, theirs, mine)
        stores.append(pltpu.make_async_copy(head_ref.at[i], head_any.at[i], sems.at[2 * i + 1]))
        stores[-1].start()
    for store in stores:
        store.wait()


def join(mine, theirs, core):
    conv, head = (OFFS + 1, 128, 256), (9, 256, 128)
    return pl.pallas_call(
        final_kernel,
        out_shape=[jax.ShapeDtypeStruct(conv, F32), jax.ShapeDtypeStruct(head, F32)],
        in_specs=[VMEM, VMEM, SMEM],
        out_specs=[ANY, ANY],
        scratch_shapes=[pltpu.VMEM(conv, F32), pltpu.VMEM(head, F32), pltpu.SemaphoreType.DMA((18,))],
        compiler_params=pltpu.CompilerParams(vmem_limit_bytes=32 * 1024 * 1024),
    )(mine, theirs, core)


def chain(block, axes, by):
    count = lax.axis_size(axes)
    return lax.ppermute(
        block, axes, [(i, i + by) for i in range(count) if 0 <= i + by < count]
    )


def swap(block):
    return lax.ppermute(block, "c", [(0, 1), (1, 0)])


def exchange(block, axes):
    return lax.all_to_all(block, axes, split_axis=0, concat_axis=0, tiled=True)


def local(
    points,
    point_brick,
    point_voxel,
    send_rows,
    pair_in,
    pair_out,
    bev_cell,
    conv_weight,
    head_weight,
    head_cot,
):
    shape = jax.ShapeDtypeStruct
    voxels = bev_cell.shape[2]
    total = points.shape[0]
    core = jnp.stack([lax.axis_index("c"), lax.axis_index("y")]).astype(I32)

    ready = call(
        fill_kernel,
        shape((128, ROWS, 128), BF),
        (point_brick.reshape(1, total), point_voxel.reshape(1, total), points),
        scratch=[pltpu.VMEM((1, total), I32)],
        flops=3 << 30,
    )
    cot = head_cot.reshape(-1, 128)
    cells = cot.shape[0]
    cot_low = chain(cot[cells - 64 :], PLANE, 1)
    cot_high = chain(cot[:64], PLANE, -1)
    got = exchange(ready, ALL)

    window, upstream = call(
        window_kernel,
        [shape((voxels, 9 * 128), BF), shape((voxels, 256), BF)],
        (bev_cell.reshape(voxels), cot_low, cot, cot_high, head_weight),
        specs=[SMEM] + [VMEM] * 4,
        scratch=[pltpu.VMEM((66, 80, 128), F32), pltpu.VMEM((3, 4 * voxels, 128), F32)],
        flops=1 << 30,
    )

    got, window, upstream = lax.optimization_barrier((got, window, upstream))

    sides = send_rows[0, 0]
    even = core[0] == 0
    sides = jnp.concatenate(
        [sides[:2], jnp.where(even, sides[3:], sides[2:3]), jnp.where(even, sides[2:3], sides[3:])]
    )
    pooled, outgoing = call(
        pool_kernel,
        [shape((voxels, 128), BF), shape((256, 128), BF)],
        (got, sides.reshape(256, 1)),
        scratch=[pltpu.VMEM((voxels, 128), F32)],
        flops=2 << 30,
    )
    layers = lax.axis_size(HEIGHT)
    pairs = [(i, i + 1) for i in range(1, layers - 1, 2)]
    from_left = chain(outgoing[64:128], PLANE, 1)
    from_right = chain(outgoing[0:64], PLANE, -1)
    paired = lax.ppermute(outgoing[192:256], HEIGHT, pairs + [(j, i) for i, j in pairs])
    swapped = swap(outgoing[128:192])
    table_width = (OFFS + 1) * 128
    grad_rows = table_width + 9 * 128
    act, keep, send = call(
        conv_kernel,
        [shape((voxels, 256), BF), shape((grad_rows, 128), BF), shape((grad_rows, 128), BF)],
        (
            core,
            pooled,
            from_left,
            from_right,
            swapped,
            paired,
            jnp.transpose(pair_in[0, 0]),
            pair_out[0, 0],
            conv_weight.reshape(table_width, 256),
            upstream,
            window,
        ),
        specs=[SMEM] + [VMEM] * 7 + [ANY] * 3,
        out=ANY,
        scratch=[
            pltpu.VMEM((256, 5 * 128), BF),
            pltpu.VMEM((OFFS * 256, 128), BF),
            pltpu.VMEM((voxels, table_width), BF),
            pltpu.VMEM((256, voxels), BF),
            pltpu.VMEM((table_width, 256), BF),
            pltpu.VMEM((voxels, 256), BF),
            pltpu.VMEM((voxels, 9 * 128), BF),
            pltpu.VMEM((voxels, 256), BF),
            pltpu.VMEM((grad_rows, 128), BF),
            pltpu.VMEM((grad_rows, 128), BF),
            pltpu.SemaphoreType.DMA((8,)),
        ],
        flops=8 << 30,
        limit=60,
    )

    both = (keep.astype(F32) + swap(send).astype(F32)).astype(BF)
    both, act = lax.optimization_barrier((both, act))
    shares = exchange(both.reshape(16, grad_rows // 16, 128), PLANE)
    share = jnp.sum(shares.astype(F32), axis=0).astype(BF)
    shares = exchange(jnp.broadcast_to(share[None], (4,) + share.shape), "y")
    share = jnp.sum(shares.astype(F32), axis=0).astype(BF)
    head_keep, head_send = call(
        head_kernel,
        [shape((4 * EDGED, 128), BF), shape((4 * EDGED, 128), BF)],
        (core, bev_cell.reshape(1, voxels), act, head_weight),
        specs=[SMEM, VMEM, VMEM, VMEM],
        scratch=[pltpu.VMEM((3, 256, 384), BF), pltpu.VMEM((66 * 64, 128), F32)],
        flops=4 << 30,
    )
    head = (head_keep.astype(F32) + swap(head_send).astype(F32)).astype(BF)
    mine = exchange(jnp.broadcast_to(share[None], (16,) + share.shape), PLANE).reshape(36, 128, 128)
    total = head[:EDGED].astype(F32)
    for d in (1, 2, 3):
        sent = head[d * EDGED : (d + 1) * EDGED]
        total = total + lax.ppermute(sent, "y", [(i, (i + d) % 4) for i in range(4)]).astype(F32)
    tiles = lax.axis_size(PLANE)
    ends = [(t * layers - 1, t * layers) for t in range(1, tiles)]
    beyond = lax.ppermute(total[512:].astype(BF), ALL, ends + [(j, i) for i, j in ends]).astype(F32)
    layer = lax.axis_index(HEIGHT)
    head_out = jnp.concatenate(
        [
            total[:64] + jnp.where(layer == 0, beyond, 0.0),
            total[64:448],
            total[448:512] + jnp.where(layer == layers - 1, beyond, 0.0),
        ]
    ).astype(BF)
    mine, head_out = lax.optimization_barrier((mine, head_out))
    conv_grad, head_grad = join(mine, swap(mine), core)
    return (head_out.reshape(8, 64, 128), conv_grad, head_grad)


def solution(mesh):
    grid = Mesh(mesh.devices.reshape(4, 4, 4, 2), ALL)
    in_specs = (
        P(ALL, None),
        P(ALL, None),
        P(ALL),
        P(PLANE, HEIGHT, None, None),
        P(PLANE, HEIGHT, None, None),
        P(PLANE, HEIGHT, None, None),
        P(PLANE, HEIGHT, None),
        P(),
        P(),
        P(PLANE, None, None),
    )
    out_specs = (P(ALL, None, None), P(), P())
    return jax.shard_map(local, mesh=grid, in_specs=in_specs, out_specs=out_specs, check_vma=False)
```

```python
import functools

import jax
import jax.numpy as jnp
from jax import lax
from jax.experimental import pallas as pl
from jax.experimental.pallas import tpu as pltpu
from jax.sharding import Mesh, PartitionSpec as P

BF = jnp.bfloat16
F32 = jnp.float32
I32 = jnp.int32
PLANE = ("x", "z")
HEIGHT = ("y", "c")
ALL = ("x", "z", "y", "c")
CAP = 32
ROWS = 40
OFFS = 26
EDGED = 576
VMEM = pl.BlockSpec(memory_space=pltpu.VMEM)
SMEM = pl.BlockSpec(memory_space=pltpu.SMEM)
ANY = pl.BlockSpec(memory_space=pl.ANY)


def iota(shape, axis):
    return lax.broadcasted_iota(I32, shape, axis)


def hot(mask):
    return jnp.where(mask, 1.0, 0.0).astype(BF)


def dot(a, b):
    return jnp.dot(a, b, preferred_element_type=F32)


def dot_rows(a, b):
    return lax.dot_general(a, b, (((0,), (0,)), ((), ())), preferred_element_type=F32)


def dot_lanes(a, b):
    return lax.dot_general(a, b, (((1,), (1,)), ((), ())), preferred_element_type=F32)


def call(kernel, outs, args, specs=None, scratch=(), flops=0, limit=56, out=VMEM):
    return pl.pallas_call(
        kernel,
        out_shape=outs,
        in_specs=[VMEM] * len(args) if specs is None else specs,
        out_specs=jax.tree.map(lambda _: out, outs),
        scratch_shapes=list(scratch),
        compiler_params=pltpu.CompilerParams(vmem_limit_bytes=limit * 1024 * 1024),
        cost_estimate=pl.CostEstimate(flops=flops, bytes_accessed=4 << 20, transcendentals=0),
    )(*args)


def fill_kernel(brick_ref, voxel_ref, points_ref, out_ref, slot_ref):
    step = 256
    total = brick_ref.shape[1]
    upper = hot(iota((step, step), 0) <= iota((step, step), 1))
    spans = [slice(first, first + step) for first in range(0, total, step)]
    masks = [brick_ref[:, span] == iota((128, step), 0) for span in spans]
    counts = dot(jnp.concatenate([hot(mask) for mask in masks], axis=0), upper)
    before = jnp.zeros((128, 1), F32)
    ranks = []
    for i, span in enumerate(spans):
        count = counts[i * 128 : (i + 1) * 128]
        rank = jnp.sum(jnp.where(masks[i], count + (before - 1.0), 0.0), axis=0, keepdims=True)
        before = before + count[:, step - 1 :]
        slot_ref[:, span] = brick_ref[:, span] * CAP + rank.astype(I32)
        ranks.append(rank.astype(I32))
    rank = jnp.concatenate(ranks, axis=1)
    member = brick_ref[...] == iota((128, total), 0)
    voxel = voxel_ref[...]
    high = jnp.where(member, (voxel >> 5).astype(F32), 0.0).astype(BF)
    low = jnp.where(member, (voxel & 31).astype(F32), 0.0).astype(BF)
    by_rank = hot(rank == (iota((128, total), 0) & (CAP - 1)))
    codes = dot_lanes(jnp.concatenate([high, low], axis=0), by_rank)
    place = iota((128, ROWS - CAP, 128), 1)
    rows = jnp.where(place == 0, codes[:128][:, None, :], 0.0)
    rows = jnp.where(place == 1, codes[128:][:, None, :], rows)
    out_ref[:, CAP:ROWS, :] = rows.astype(BF)
    for m in range(0, 128 * CAP, 512):
        match = hot(slot_ref[...] == iota((512, total), 0) + m)
        rows = dot(match, points_ref[...]).astype(BF)
        out_ref[m // CAP : (m + 512) // CAP, 0:CAP, :] = rows.reshape(512 // CAP, CAP, 128)


def pool_kernel(got_ref, rim_ref, pooled_ref, rows_ref, acc_ref):
    voxels = pooled_ref.shape[0]
    own = (iota((8, 256), 1) >> 5) == iota((8, 256), 0)
    for i in range(16):
        codes = got_ref[i * 8 : i * 8 + 8, CAP:ROWS, :].astype(F32)
        ids = codes[:, 0, :] * 32.0 + codes[:, 1, :]
        wide = jnp.concatenate([ids, ids], axis=1)
        row = jnp.sum(jnp.where(own, wide, 0.0), axis=0, keepdims=True).astype(I32)
        match = hot(row == iota((voxels, 256), 0))
        part = dot(match, got_ref[i * 8 : i * 8 + 8, 0:CAP, :].reshape(256, 128))
        acc_ref[...] = part if i == 0 else acc_ref[...] + part
    pooled = acc_ref[...].astype(BF)
    pooled_ref[...] = pooled
    rows_ref[...] = dot(hot(rim_ref[...] == iota((256, voxels), 1)), pooled).astype(BF)


def shifts(rows):
    total = rows.shape[0]
    y = iota(rows.shape, 0)
    wide = rows.astype(F32)
    lower = jnp.where(y == 0, 0.0, pltpu.roll(wide, 1, 0))
    upper = jnp.where(y == total - 1, 0.0, pltpu.roll(wide, total - 1, 0))
    return [lower.astype(BF), rows, upper.astype(BF)]


def conv_kernel(
    core_ref,
    pooled_ref,
    left_ref,
    right_ref,
    swapped_ref,
    paired_ref,
    src_ref,
    dst_ref,
    low_ref,
    high_ref,
    cell_ref,
    head_ref,
    weight_any,
    upstream_any,
    window_any,
    act_any,
    keep_any,
    send_any,
    wide_ref,
    rows_ref,
    table_ref,
    grad_ref,
    weight_ref,
    upstream_ref,
    window_ref,
    act_ref,
    keep_ref,
    send_ref,
    edge_ref,
    sems,
):
    voxels = pooled_ref.shape[0]
    loads = [
        pltpu.make_async_copy(weight_any, weight_ref, sems.at[0]),
        pltpu.make_async_copy(upstream_any, upstream_ref, sems.at[1]),
        pltpu.make_async_copy(window_any, window_ref, sems.at[2]),
    ]
    for load in loads:
        load.start()
    first = core_ref[0] == 0
    for g in range(4):
        wide_ref[:, g * 128 : (g + 1) * 128] = pooled_ref[g * 256 : (g + 1) * 256, :]
    swapped, paired = swapped_ref[...].astype(F32), paired_ref[...].astype(F32)
    wide_ref[0:64, 512:640] = left_ref[...]
    wide_ref[64:128, 512:640] = right_ref[...]
    wide_ref[128:192, 512:640] = jnp.where(first, paired, swapped).astype(BF)
    wide_ref[192:256, 512:640] = jnp.where(first, swapped, paired).astype(BF)
    row = src_ref[...] & 255
    group = src_ref[...] >> 8
    for k in range(OFFS):
        rows = dot(hot(row[:, k : k + 1] == iota((256, 256), 1)), wide_ref[...])
        side = jnp.broadcast_to(group[:, k : k + 1], (256, 128))
        picked = jnp.zeros((256, 128), F32)
        for g in range(5):
            picked = jnp.where(side == g, rows[:, g * 128 : (g + 1) * 128], picked)
        rows_ref[k * 256 : (k + 1) * 256, :] = picked.astype(BF)
    for k in range(OFFS):
        place = hot(dst_ref[k : k + 1, :] == iota((voxels, 256), 0))
        table_ref[:, k * 128 : (k + 1) * 128] = dot(place, rows_ref[k * 256 : (k + 1) * 256, :]).astype(BF)
    table_ref[:, OFFS * 128 :] = pooled_ref[...]
    edge_ref[...] = jnp.zeros_like(edge_ref)
    lows, highs = shifts(low_ref[...]), shifts(high_ref[...])
    reach = jnp.zeros((128, 256), F32)
    for b in range(3):
        edge_ref[64:128, b * 128 : (b + 1) * 128] = highs[2 - b]
        edge_ref[0:64, (3 + b) * 128 : (4 + b) * 128] = lows[2 - b]
    for a in range(2):
        for b in range(3):
            k = 3 * a + b
            reach = reach + dot_lanes(edge_ref[:, k * 128 : (k + 1) * 128], head_ref[6 * a + b])
    edge_row = iota((128, voxels), 0)
    at_edge = hot(cell_ref[...] == jnp.where(edge_row < 64, edge_row, edge_row + (63 * 64 - 64)))
    coarse = reach.astype(BF)
    fine = (reach - coarse.astype(F32)).astype(BF)
    loads[0].wait()
    loads[1].wait()
    upstream_ref[...] += dot_rows(at_edge, coarse) + dot_rows(at_edge, fine)
    loads[2].wait()
    beside = dot_rows(at_edge, edge_ref[...])
    for a in range(2):
        span = slice(a * 768, a * 768 + 384)
        window_ref[:, span] = (window_ref[:, span].astype(F32) + beside[:, a * 384 : (a + 1) * 384]).astype(BF)
    for m in range(0, voxels, 512):
        pre = dot(table_ref[m : m + 512, :], weight_ref[...])
        sigma = 1.0 / (1.0 + jnp.exp(-pre))
        act_ref[m : m + 512, :] = (pre * sigma).astype(BF)
        slope = sigma * (1.0 + pre * (1.0 - sigma))
        grad = upstream_ref[m : m + 512, :].astype(BF).astype(F32) * slope
        grad_ref[:, m : m + 512] = grad.T.astype(BF)
    stores = [pltpu.make_async_copy(act_ref, act_any, sems.at[3])]
    stores[0].start()
    wide = 9 * 128
    for step in range(3):
        full = dot(grad_ref[...], table_ref[:, step * wide : (step + 1) * wide])
        for at in range(0, wide, 128):
            lo, hi = full[:128, at : at + 128], full[128:, at : at + 128]
            to = step * wide + at
            keep_ref[to : to + 128, :] = jnp.where(first, lo, hi).T.astype(BF)
            send_ref[to : to + 128, :] = jnp.where(first, hi, lo).T.astype(BF)
    base = (OFFS + 1) * 128
    stores += [
        pltpu.make_async_copy(send_ref.at[0:base], send_any.at[0:base], sems.at[4]),
        pltpu.make_async_copy(keep_ref.at[0:base], keep_any.at[0:base], sems.at[5]),
    ]
    stores[1].start()
    stores[2].start()
    full = dot_rows(act_ref[...], window_ref[...])
    for at in range(0, wide, 128):
        lo, hi = full[:128, at : at + 128], full[128:, at : at + 128]
        keep_ref[base + at : base + at + 128, :] = jnp.where(first, lo, hi).astype(BF)
        send_ref[base + at : base + at + 128, :] = jnp.where(first, hi, lo).astype(BF)
    stores += [
        pltpu.make_async_copy(send_ref.at[base : base + wide], send_any.at[base : base + wide], sems.at[6]),
        pltpu.make_async_copy(keep_ref.at[base : base + wide], keep_any.at[base : base + wide], sems.at[7]),
    ]
    stores[3].start()
    stores[4].start()
    for store in stores:
        store.wait()


def head_kernel(core_ref, cell_ref, act_ref, weight_ref, keep_ref, send_ref, wide_ref, total_ref):
    core, here = core_ref[0], core_ref[1]
    for a in range(3):
        for b in range(3):
            wide_ref[b, :, a * 128 : (a + 1) * 128] = weight_ref[3 * a + b]
    total_ref[...] = jnp.zeros_like(total_ref)
    y = iota((512, 256), 0) & 63
    for part in range(8):
        match = hot(cell_ref[...] - part * 512 == iota((512, cell_ref.shape[1]), 0))
        column = dot(match, act_ref[...])
        lower = jnp.where(y == 0, 0.0, pltpu.roll(column, 1, 0)).astype(BF)
        upper = jnp.where(y == 63, 0.0, pltpu.roll(column, 511, 0)).astype(BF)
        rows = dot(lower, wide_ref[0]) + dot(column.astype(BF), wide_ref[1]) + dot(upper, wide_ref[2])
        for a in range(3):
            at = (part * 8 + 2 - a) * 64
            total_ref[at : at + 512, :] += rows[:, a * 128 : (a + 1) * 128]
    for d in range(4):
        for out_ref, which in ((send_ref, 1 - core), (keep_ref, core)):
            layer = ((here + d) & 3) * 2 + which
            first = pl.multiple_of(layer * 512 + 64, 64)
            out_ref[d * EDGED : d * EDGED + 512, :] = total_ref[pl.ds(first, 512), :].astype(BF)
            beyond = jnp.where(layer == 7, total_ref[65 * 64 : 66 * 64, :], 0.0)
            beyond = jnp.where(layer == 0, total_ref[0:64, :], beyond)
            out_ref[d * EDGED + 512 : (d + 1) * EDGED, :] = beyond.astype(BF)


def window_kernel(cell_ref, cot_ref, weight_ref, window_ref, up_ref, pad_ref, rows_ref):
    voxels = window_ref.shape[0]
    pad_ref[:, 0:8, :] = jnp.zeros((66, 8, 128), F32)
    pad_ref[:, 72:80, :] = jnp.zeros((66, 8, 128), F32)
    pad_ref[0, 8:72, :] = jnp.zeros((64, 128), F32)
    pad_ref[1:65, 8:72, :] = cot_ref[...].reshape(64, 64, 128).astype(F32)
    pad_ref[65, 8:72, :] = jnp.zeros((64, 128), F32)

    def step_window(v, carry):
        cell = cell_ref[v]
        x = cell >> 6
        y = (cell & 63) + 7
        for a in range(3):
            rows_ref[a, pl.ds(v * 4, 4), :] = pad_ref[x + (2 - a), pl.ds(y, 4), :]
        return carry

    lax.fori_loop(0, voxels, step_window, 0, unroll=16)
    up = jnp.zeros(up_ref.shape, F32)
    for a in range(3):
        for b in range(3):
            k = 3 * a + b
            rows = rows_ref[a, pl.ds(2 - b, voxels, stride=4), :].astype(BF)
            window_ref[:, k * 128 : (k + 1) * 128] = rows
            up = up + dot_lanes(rows, weight_ref[k])
    up_ref[...] = up


def final_kernel(mine_ref, theirs_ref, core_ref, conv_any, head_any, conv_ref, head_ref, sems):
    first = core_ref[0] == 0
    stores = []
    for i in range(9):
        for k in range(3 * i, 3 * i + 3):
            mine, theirs = mine_ref[k].astype(F32), theirs_ref[k].astype(F32)
            conv_ref[k, :, 0:128] = jnp.where(first, mine, theirs)
            conv_ref[k, :, 128:256] = jnp.where(first, theirs, mine)
        part = pl.ds(3 * i, 3)
        stores.append(pltpu.make_async_copy(conv_ref.at[part], conv_any.at[part], sems.at[2 * i]))
        stores[-1].start()
        mine, theirs = mine_ref[OFFS + 1 + i].astype(F32), theirs_ref[OFFS + 1 + i].astype(F32)
        head_ref[i, 0:128, :] = jnp.where(first, mine, theirs)
        head_ref[i, 128:256, :] = jnp.where(first, theirs, mine)
        stores.append(pltpu.make_async_copy(head_ref.at[i], head_any.at[i], sems.at[2 * i + 1]))
        stores[-1].start()
    for store in stores:
        store.wait()


def join(mine, theirs, core):
    conv, head = (OFFS + 1, 128, 256), (9, 256, 128)
    return pl.pallas_call(
        final_kernel,
        out_shape=[jax.ShapeDtypeStruct(conv, F32), jax.ShapeDtypeStruct(head, F32)],
        in_specs=[VMEM, VMEM, SMEM],
        out_specs=[ANY, ANY],
        scratch_shapes=[pltpu.VMEM(conv, F32), pltpu.VMEM(head, F32), pltpu.SemaphoreType.DMA((18,))],
        compiler_params=pltpu.CompilerParams(vmem_limit_bytes=32 * 1024 * 1024),
    )(mine, theirs, core)


def chain(block, axes, by):
    count = lax.axis_size(axes)
    return lax.ppermute(
        block, axes, [(i, i + by) for i in range(count) if 0 <= i + by < count]
    )


def swap(block):
    return lax.ppermute(block, "c", [(0, 1), (1, 0)])


def exchange(block, axes):
    return lax.all_to_all(block, axes, split_axis=0, concat_axis=0, tiled=True)


def local(
    points,
    point_brick,
    point_voxel,
    send_rows,
    pair_in,
    pair_out,
    bev_cell,
    conv_weight,
    head_weight,
    head_cot,
):
    shape = jax.ShapeDtypeStruct
    voxels = bev_cell.shape[2]
    total = points.shape[0]
    core = jnp.stack([lax.axis_index("c"), lax.axis_index("y")]).astype(I32)

    ready = call(
        fill_kernel,
        shape((128, ROWS, 128), BF),
        (point_brick.reshape(1, total), point_voxel.reshape(1, total), points),
        scratch=[pltpu.VMEM((1, total), I32)],
        flops=3 << 30,
    )
    cot = head_cot.reshape(-1, 128)
    cells = cot.shape[0]
    cot_low = chain(cot[cells - 64 :], PLANE, 1)
    cot_high = chain(cot[:64], PLANE, -1)
    got = exchange(ready, ALL)

    window, upstream = call(
        window_kernel,
        [shape((voxels, 9 * 128), BF), shape((voxels, 256), F32)],
        (bev_cell.reshape(voxels), cot, head_weight),
        specs=[SMEM] + [VMEM] * 2,
        scratch=[pltpu.VMEM((66, 80, 128), F32), pltpu.VMEM((3, 4 * voxels, 128), F32)],
        flops=1 << 30,
    )

    got, window, upstream = lax.optimization_barrier((got, window, upstream))

    sides = send_rows[0, 0]
    even = core[0] == 0
    sides = jnp.concatenate(
        [sides[:2], jnp.where(even, sides[3:], sides[2:3]), jnp.where(even, sides[2:3], sides[3:])]
    )
    pooled, outgoing = call(
        pool_kernel,
        [shape((voxels, 128), BF), shape((256, 128), BF)],
        (got, sides.reshape(256, 1)),
        scratch=[pltpu.VMEM((voxels, 128), F32)],
        flops=2 << 30,
    )
    layers = lax.axis_size(HEIGHT)
    pairs = [(i, i + 1) for i in range(1, layers - 1, 2)]
    from_left = chain(outgoing[64:128], PLANE, 1)
    from_right = chain(outgoing[0:64], PLANE, -1)
    paired = lax.ppermute(outgoing[192:256], HEIGHT, pairs + [(j, i) for i, j in pairs])
    swapped = swap(outgoing[128:192])
    table_width = (OFFS + 1) * 128
    grad_rows = table_width + 9 * 128
    act, keep, send = call(
        conv_kernel,
        [shape((voxels, 256), BF), shape((grad_rows, 128), BF), shape((grad_rows, 128), BF)],
        (
            core,
            pooled,
            from_left,
            from_right,
            swapped,
            paired,
            jnp.transpose(pair_in[0, 0]),
            pair_out[0, 0],
            cot_low,
            cot_high,
            bev_cell.reshape(1, voxels),
            head_weight,
            conv_weight.reshape(table_width, 256),
            upstream,
            window,
        ),
        specs=[SMEM] + [VMEM] * 11 + [ANY] * 3,
        out=ANY,
        scratch=[
            pltpu.VMEM((256, 5 * 128), BF),
            pltpu.VMEM((OFFS * 256, 128), BF),
            pltpu.VMEM((voxels, table_width), BF),
            pltpu.VMEM((256, voxels), BF),
            pltpu.VMEM((table_width, 256), BF),
            pltpu.VMEM((voxels, 256), F32),
            pltpu.VMEM((voxels, 9 * 128), BF),
            pltpu.VMEM((voxels, 256), BF),
            pltpu.VMEM((grad_rows, 128), BF),
            pltpu.VMEM((grad_rows, 128), BF),
            pltpu.VMEM((128, 6 * 128), BF),
            pltpu.SemaphoreType.DMA((8,)),
        ],
        flops=8 << 30,
        limit=60,
    )

    both = (keep.astype(F32) + swap(send).astype(F32)).astype(BF)
    both, act = lax.optimization_barrier((both, act))
    shares = exchange(both.reshape(16, grad_rows // 16, 128), PLANE)
    share = jnp.sum(shares.astype(F32), axis=0).astype(BF)
    shares = exchange(jnp.broadcast_to(share[None], (4,) + share.shape), "y")
    share = jnp.sum(shares.astype(F32), axis=0).astype(BF)
    head_keep, head_send = call(
        head_kernel,
        [shape((4 * EDGED, 128), BF), shape((4 * EDGED, 128), BF)],
        (core, bev_cell.reshape(1, voxels), act, head_weight),
        specs=[SMEM, VMEM, VMEM, VMEM],
        scratch=[pltpu.VMEM((3, 256, 384), BF), pltpu.VMEM((66 * 64, 128), F32)],
        flops=4 << 30,
    )
    head = (head_keep.astype(F32) + swap(head_send).astype(F32)).astype(BF)
    mine = exchange(jnp.broadcast_to(share[None], (16,) + share.shape), PLANE).reshape(36, 128, 128)
    total = head[:EDGED].astype(F32)
    for d in (1, 2, 3):
        sent = head[d * EDGED : (d + 1) * EDGED]
        total = total + lax.ppermute(sent, "y", [(i, (i + d) % 4) for i in range(4)]).astype(F32)
    tiles = lax.axis_size(PLANE)
    ends = [(t * layers - 1, t * layers) for t in range(1, tiles)]
    beyond = lax.ppermute(total[512:].astype(BF), ALL, ends + [(j, i) for i, j in ends]).astype(F32)
    layer = lax.axis_index(HEIGHT)
    head_out = jnp.concatenate(
        [
            total[:64] + jnp.where(layer == 0, beyond, 0.0),
            total[64:448],
            total[448:512] + jnp.where(layer == layers - 1, beyond, 0.0),
        ]
    ).astype(BF)
    mine, head_out = lax.optimization_barrier((mine, head_out))
    conv_grad, head_grad = join(mine, swap(mine), core)
    return (head_out.reshape(8, 64, 128), conv_grad, head_grad)


def solution(mesh):
    grid = Mesh(mesh.devices.reshape(4, 4, 4, 2), ALL)
    in_specs = (
        P(ALL, None),
        P(ALL, None),
        P(ALL),
        P(PLANE, HEIGHT, None, None),
        P(PLANE, HEIGHT, None, None),
        P(PLANE, HEIGHT, None, None),
        P(PLANE, HEIGHT, None),
        P(),
        P(),
        P(PLANE, None, None),
    )
    out_specs = (P(ALL, None, None), P(), P())
    return jax.shard_map(local, mesh=grid, in_specs=in_specs, out_specs=out_specs, check_vma=False)
```

```python
import functools

import jax
import jax.numpy as jnp
from jax import lax
from jax.experimental import pallas as pl
from jax.experimental.pallas import tpu as pltpu
from jax.sharding import Mesh, PartitionSpec as P

BF = jnp.bfloat16
F32 = jnp.float32
I32 = jnp.int32
PLANE = ("x", "z")
HEIGHT = ("y", "c")
ALL = ("x", "z", "y", "c")
CAP = 32
ROWS = 40
OFFS = 26
EDGED = 576
VMEM = pl.BlockSpec(memory_space=pltpu.VMEM)
SMEM = pl.BlockSpec(memory_space=pltpu.SMEM)
ANY = pl.BlockSpec(memory_space=pl.ANY)


def iota(shape, axis):
    return lax.broadcasted_iota(I32, shape, axis)


def hot(mask):
    return jnp.where(mask, 1.0, 0.0).astype(BF)


def dot(a, b):
    return jnp.dot(a, b, preferred_element_type=F32)


def dot_rows(a, b):
    return lax.dot_general(a, b, (((0,), (0,)), ((), ())), preferred_element_type=F32)


def dot_lanes(a, b):
    return lax.dot_general(a, b, (((1,), (1,)), ((), ())), preferred_element_type=F32)


def call(kernel, outs, args, specs=None, scratch=(), flops=0, limit=56, out=VMEM):
    return pl.pallas_call(
        kernel,
        out_shape=outs,
        in_specs=[VMEM] * len(args) if specs is None else specs,
        out_specs=jax.tree.map(lambda _: out, outs),
        scratch_shapes=list(scratch),
        compiler_params=pltpu.CompilerParams(vmem_limit_bytes=limit * 1024 * 1024),
        cost_estimate=pl.CostEstimate(flops=flops, bytes_accessed=4 << 20, transcendentals=0),
    )(*args)


def fill_kernel(brick_ref, voxel_ref, points_ref, out_ref, slot_ref):
    step = 256
    total = brick_ref.shape[1]
    upper = hot(iota((step, step), 0) <= iota((step, step), 1))
    spans = [slice(first, first + step) for first in range(0, total, step)]
    masks = [brick_ref[:, span] == iota((128, step), 0) for span in spans]
    counts = dot(jnp.concatenate([hot(mask) for mask in masks], axis=0), upper)
    before = jnp.zeros((128, 1), F32)
    ranks = []
    for i, span in enumerate(spans):
        count = counts[i * 128 : (i + 1) * 128]
        rank = jnp.sum(jnp.where(masks[i], count + (before - 1.0), 0.0), axis=0, keepdims=True)
        before = before + count[:, step - 1 :]
        slot_ref[:, span] = brick_ref[:, span] * CAP + rank.astype(I32)
        ranks.append(rank.astype(I32))
    rank = jnp.concatenate(ranks, axis=1)
    member = brick_ref[...] == iota((128, total), 0)
    voxel = voxel_ref[...]
    high = jnp.where(member, (voxel >> 5).astype(F32), 0.0).astype(BF)
    low = jnp.where(member, (voxel & 31).astype(F32), 0.0).astype(BF)
    by_rank = hot(rank == (iota((128, total), 0) & (CAP - 1)))
    codes = dot_lanes(jnp.concatenate([high, low], axis=0), by_rank)
    place = iota((128, ROWS - CAP, 128), 1)
    rows = jnp.where(place == 0, codes[:128][:, None, :], 0.0)
    rows = jnp.where(place == 1, codes[128:][:, None, :], rows)
    out_ref[:, CAP:ROWS, :] = rows.astype(BF)
    for m in range(0, 128 * CAP, 512):
        match = hot(slot_ref[...] == iota((512, total), 0) + m)
        rows = dot(match, points_ref[...]).astype(BF)
        out_ref[m // CAP : (m + 512) // CAP, 0:CAP, :] = rows.reshape(512 // CAP, CAP, 128)


def pool_kernel(got_ref, rim_ref, pooled_ref, right_ref, left_ref, swap_ref, pair_ref, acc_ref):
    voxels = pooled_ref.shape[0]
    own = (iota((8, 256), 1) >> 5) == iota((8, 256), 0)
    for i in range(16):
        codes = got_ref[i * 8 : i * 8 + 8, CAP:ROWS, :].astype(F32)
        ids = codes[:, 0, :] * 32.0 + codes[:, 1, :]
        wide = jnp.concatenate([ids, ids], axis=1)
        row = jnp.sum(jnp.where(own, wide, 0.0), axis=0, keepdims=True).astype(I32)
        match = hot(row == iota((voxels, 256), 0))
        part = dot(match, got_ref[i * 8 : i * 8 + 8, 0:CAP, :].reshape(256, 128))
        acc_ref[...] = part if i == 0 else acc_ref[...] + part
    pooled = acc_ref[...].astype(BF)
    pooled_ref[...] = pooled
    rows = dot(hot(rim_ref[...] == iota((256, voxels), 1)), pooled).astype(BF)
    for side, ref in enumerate((right_ref, left_ref, swap_ref, pair_ref)):
        ref[...] = rows[side * 64 : (side + 1) * 64]


def shifts(rows):
    total = rows.shape[0]
    y = iota(rows.shape, 0)
    wide = rows.astype(F32)
    lower = jnp.where(y == 0, 0.0, pltpu.roll(wide, 1, 0))
    upper = jnp.where(y == total - 1, 0.0, pltpu.roll(wide, total - 1, 0))
    return [lower.astype(BF), rows, upper.astype(BF)]


def conv_kernel(
    core_ref,
    pooled_ref,
    left_ref,
    right_ref,
    swapped_ref,
    paired_ref,
    src_ref,
    dst_ref,
    low_ref,
    high_ref,
    cell_ref,
    head_ref,
    weight_any,
    upstream_any,
    window_any,
    act_any,
    keep_any,
    send_any,
    wide_ref,
    rows_ref,
    table_ref,
    grad_ref,
    weight_ref,
    upstream_ref,
    window_ref,
    act_ref,
    keep_ref,
    send_ref,
    edge_ref,
    sems,
):
    voxels = pooled_ref.shape[0]
    loads = [
        pltpu.make_async_copy(weight_any, weight_ref, sems.at[0]),
        pltpu.make_async_copy(upstream_any, upstream_ref, sems.at[1]),
        pltpu.make_async_copy(window_any, window_ref, sems.at[2]),
    ]
    for load in loads:
        load.start()
    first = core_ref[0] == 0
    for g in range(4):
        wide_ref[:, g * 128 : (g + 1) * 128] = pooled_ref[g * 256 : (g + 1) * 256, :]
    swapped, paired = swapped_ref[...].astype(F32), paired_ref[...].astype(F32)
    wide_ref[0:64, 512:640] = left_ref[...]
    wide_ref[64:128, 512:640] = right_ref[...]
    wide_ref[128:192, 512:640] = jnp.where(first, paired, swapped).astype(BF)
    wide_ref[192:256, 512:640] = jnp.where(first, swapped, paired).astype(BF)
    row = src_ref[...] & 255
    group = src_ref[...] >> 8
    for k in range(OFFS):
        rows = dot(hot(row[:, k : k + 1] == iota((256, 256), 1)), wide_ref[...])
        side = jnp.broadcast_to(group[:, k : k + 1], (256, 128))
        picked = jnp.zeros((256, 128), F32)
        for g in range(5):
            picked = jnp.where(side == g, rows[:, g * 128 : (g + 1) * 128], picked)
        rows_ref[k * 256 : (k + 1) * 256, :] = picked.astype(BF)
    for k in range(OFFS):
        place = hot(dst_ref[k : k + 1, :] == iota((voxels, 256), 0))
        table_ref[:, k * 128 : (k + 1) * 128] = dot(place, rows_ref[k * 256 : (k + 1) * 256, :]).astype(BF)
    table_ref[:, OFFS * 128 :] = pooled_ref[...]
    edge_ref[...] = jnp.zeros_like(edge_ref)
    lows, highs = shifts(low_ref[...]), shifts(high_ref[...])
    reach = jnp.zeros((128, 256), F32)
    for b in range(3):
        edge_ref[64:128, b * 128 : (b + 1) * 128] = highs[2 - b]
        edge_ref[0:64, (3 + b) * 128 : (4 + b) * 128] = lows[2 - b]
    for a in range(2):
        for b in range(3):
            k = 3 * a + b
            reach = reach + dot_lanes(edge_ref[:, k * 128 : (k + 1) * 128], head_ref[6 * a + b])
    edge_row = iota((128, voxels), 0)
    at_edge = hot(cell_ref[...] == jnp.where(edge_row < 64, edge_row, edge_row + (63 * 64 - 64)))
    coarse = reach.astype(BF)
    fine = (reach - coarse.astype(F32)).astype(BF)
    loads[0].wait()
    loads[1].wait()
    upstream_ref[...] += dot_rows(at_edge, coarse) + dot_rows(at_edge, fine)
    loads[2].wait()
    beside = dot_rows(at_edge, edge_ref[...])
    for a in range(2):
        span = slice(a * 768, a * 768 + 384)
        window_ref[:, span] = (window_ref[:, span].astype(F32) + beside[:, a * 384 : (a + 1) * 384]).astype(BF)
    for m in range(0, voxels, 512):
        pre = dot(table_ref[m : m + 512, :], weight_ref[...])
        sigma = 1.0 / (1.0 + jnp.exp(-pre))
        act_ref[m : m + 512, :] = (pre * sigma).astype(BF)
        slope = sigma * (1.0 + pre * (1.0 - sigma))
        grad = upstream_ref[m : m + 512, :].astype(BF).astype(F32) * slope
        grad_ref[:, m : m + 512] = grad.T.astype(BF)
    stores = [pltpu.make_async_copy(act_ref, act_any, sems.at[3])]
    stores[0].start()
    wide = 9 * 128
    for step in range(3):
        full = dot(grad_ref[...], table_ref[:, step * wide : (step + 1) * wide])
        for at in range(0, wide, 128):
            lo, hi = full[:128, at : at + 128], full[128:, at : at + 128]
            to = step * wide + at
            keep_ref[to : to + 128, :] = jnp.where(first, lo, hi).T.astype(BF)
            send_ref[to : to + 128, :] = jnp.where(first, hi, lo).T.astype(BF)
    base = (OFFS + 1) * 128
    stores += [
        pltpu.make_async_copy(send_ref.at[0:base], send_any.at[0:base], sems.at[4]),
        pltpu.make_async_copy(keep_ref.at[0:base], keep_any.at[0:base], sems.at[5]),
    ]
    stores[1].start()
    stores[2].start()
    full = dot_rows(act_ref[...], window_ref[...])
    for at in range(0, wide, 128):
        lo, hi = full[:128, at : at + 128], full[128:, at : at + 128]
        keep_ref[base + at : base + at + 128, :] = jnp.where(first, lo, hi).astype(BF)
        send_ref[base + at : base + at + 128, :] = jnp.where(first, hi, lo).astype(BF)
    stores += [
        pltpu.make_async_copy(send_ref.at[base : base + wide], send_any.at[base : base + wide], sems.at[6]),
        pltpu.make_async_copy(keep_ref.at[base : base + wide], keep_any.at[base : base + wide], sems.at[7]),
    ]
    stores[3].start()
    stores[4].start()
    for store in stores:
        store.wait()


def head_kernel(core_ref, cell_ref, act_ref, weight_ref, keep_ref, send_ref, wide_ref, total_ref):
    core, here = core_ref[0], core_ref[1]
    for a in range(3):
        for b in range(3):
            wide_ref[b, :, a * 128 : (a + 1) * 128] = weight_ref[3 * a + b]
    total_ref[...] = jnp.zeros_like(total_ref)
    y = iota((512, 256), 0) & 63
    for part in range(8):
        match = hot(cell_ref[...] - part * 512 == iota((512, cell_ref.shape[1]), 0))
        column = dot(match, act_ref[...])
        lower = jnp.where(y == 0, 0.0, pltpu.roll(column, 1, 0)).astype(BF)
        upper = jnp.where(y == 63, 0.0, pltpu.roll(column, 511, 0)).astype(BF)
        rows = dot(lower, wide_ref[0]) + dot(column.astype(BF), wide_ref[1]) + dot(upper, wide_ref[2])
        for a in range(3):
            at = (part * 8 + 2 - a) * 64
            total_ref[at : at + 512, :] += rows[:, a * 128 : (a + 1) * 128]
    for d in range(4):
        for out_ref, which in ((send_ref, 1 - core), (keep_ref, core)):
            layer = ((here + d) & 3) * 2 + which
            first = pl.multiple_of(layer * 512 + 64, 64)
            out_ref[d * EDGED : d * EDGED + 512, :] = total_ref[pl.ds(first, 512), :].astype(BF)
            beyond = jnp.where(layer == 7, total_ref[65 * 64 : 66 * 64, :], 0.0)
            beyond = jnp.where(layer == 0, total_ref[0:64, :], beyond)
            out_ref[d * EDGED + 512 : (d + 1) * EDGED, :] = beyond.astype(BF)


def window_kernel(cell_ref, cot_ref, weight_ref, window_ref, up_ref, pad_ref, rows_ref):
    voxels = window_ref.shape[0]
    pad_ref[:, 0:8, :] = jnp.zeros((66, 8, 128), F32)
    pad_ref[:, 72:80, :] = jnp.zeros((66, 8, 128), F32)
    pad_ref[0, 8:72, :] = jnp.zeros((64, 128), F32)
    pad_ref[1:65, 8:72, :] = cot_ref[...].reshape(64, 64, 128).astype(F32)
    pad_ref[65, 8:72, :] = jnp.zeros((64, 128), F32)

    def step_window(v, carry):
        cell = cell_ref[v]
        x = cell >> 6
        y = (cell & 63) + 7
        for a in range(3):
            rows_ref[a, pl.ds(v * 4, 4), :] = pad_ref[x + (2 - a), pl.ds(y, 4), :]
        return carry

    lax.fori_loop(0, voxels, step_window, 0, unroll=16)
    up = jnp.zeros(up_ref.shape, F32)
    for a in range(3):
        for b in range(3):
            k = 3 * a + b
            rows = rows_ref[a, pl.ds(2 - b, voxels, stride=4), :].astype(BF)
            window_ref[:, k * 128 : (k + 1) * 128] = rows
            up = up + dot_lanes(rows, weight_ref[k])
    up_ref[...] = up


def final_kernel(mine_ref, theirs_ref, core_ref, conv_any, head_any, conv_ref, head_ref, sems):
    first = core_ref[0] == 0
    stores = []
    for i in range(9):
        for k in range(3 * i, 3 * i + 3):
            mine, theirs = mine_ref[k].astype(F32), theirs_ref[k].astype(F32)
            conv_ref[k, :, 0:128] = jnp.where(first, mine, theirs)
            conv_ref[k, :, 128:256] = jnp.where(first, theirs, mine)
        part = pl.ds(3 * i, 3)
        stores.append(pltpu.make_async_copy(conv_ref.at[part], conv_any.at[part], sems.at[2 * i]))
        stores[-1].start()
        mine, theirs = mine_ref[OFFS + 1 + i].astype(F32), theirs_ref[OFFS + 1 + i].astype(F32)
        head_ref[i, 0:128, :] = jnp.where(first, mine, theirs)
        head_ref[i, 128:256, :] = jnp.where(first, theirs, mine)
        stores.append(pltpu.make_async_copy(head_ref.at[i], head_any.at[i], sems.at[2 * i + 1]))
        stores[-1].start()
    for store in stores:
        store.wait()


def join(mine, theirs, core):
    conv, head = (OFFS + 1, 128, 256), (9, 256, 128)
    return pl.pallas_call(
        final_kernel,
        out_shape=[jax.ShapeDtypeStruct(conv, F32), jax.ShapeDtypeStruct(head, F32)],
        in_specs=[VMEM, VMEM, SMEM],
        out_specs=[ANY, ANY],
        scratch_shapes=[pltpu.VMEM(conv, F32), pltpu.VMEM(head, F32), pltpu.SemaphoreType.DMA((18,))],
        compiler_params=pltpu.CompilerParams(vmem_limit_bytes=32 * 1024 * 1024),
    )(mine, theirs, core)


def chain(block, axes, by):
    count = lax.axis_size(axes)
    return lax.ppermute(
        block, axes, [(i, i + by) for i in range(count) if 0 <= i + by < count]
    )


def swap(block):
    return lax.ppermute(block, "c", [(0, 1), (1, 0)])


def exchange(block, axes):
    return lax.all_to_all(block, axes, split_axis=0, concat_axis=0, tiled=True)


def local(
    points,
    point_brick,
    point_voxel,
    send_rows,
    pair_in,
    pair_out,
    bev_cell,
    conv_weight,
    head_weight,
    head_cot,
):
    shape = jax.ShapeDtypeStruct
    voxels = bev_cell.shape[2]
    total = points.shape[0]
    core = jnp.stack([lax.axis_index("c"), lax.axis_index("y")]).astype(I32)

    ready = call(
        fill_kernel,
        shape((128, ROWS, 128), BF),
        (point_brick.reshape(1, total), point_voxel.reshape(1, total), points),
        scratch=[pltpu.VMEM((1, total), I32)],
        flops=3 << 30,
    )
    cot = head_cot.reshape(-1, 128)
    cells = cot.shape[0]
    cot_low = chain(cot[cells - 64 :], PLANE, 1)
    cot_high = chain(cot[:64], PLANE, -1)
    got = exchange(ready, ALL)

    window, upstream = call(
        window_kernel,
        [shape((voxels, 9 * 128), BF), shape((voxels, 256), F32)],
        (bev_cell.reshape(voxels), cot, head_weight),
        specs=[SMEM] + [VMEM] * 2,
        scratch=[pltpu.VMEM((66, 80, 128), F32), pltpu.VMEM((3, 4 * voxels, 128), F32)],
        flops=1 << 30,
    )

    sources, targets = jnp.transpose(pair_in[0, 0]), pair_out[0, 0]
    got, window, upstream, sources, targets, core = lax.optimization_barrier(
        (got, window, upstream, sources, targets, core)
    )

    sides = send_rows[0, 0]
    even = core[0] == 0
    sides = jnp.concatenate(
        [sides[:2], jnp.where(even, sides[3:], sides[2:3]), jnp.where(even, sides[2:3], sides[3:])]
    )
    pooled, to_right, to_left, to_swap, to_pair = call(
        pool_kernel,
        [shape((voxels, 128), BF)] + [shape((64, 128), BF)] * 4,
        (got, sides.reshape(256, 1)),
        scratch=[pltpu.VMEM((voxels, 128), F32)],
        flops=2 << 30,
    )
    layers = lax.axis_size(HEIGHT)
    pairs = [(i, i + 1) for i in range(1, layers - 1, 2)]
    from_left = chain(to_left, PLANE, 1)
    from_right = chain(to_right, PLANE, -1)
    paired = lax.ppermute(to_pair, HEIGHT, pairs + [(j, i) for i, j in pairs])
    swapped = swap(to_swap)
    table_width = (OFFS + 1) * 128
    grad_rows = table_width + 9 * 128
    act, keep, send = call(
        conv_kernel,
        [shape((voxels, 256), BF), shape((grad_rows, 128), BF), shape((grad_rows, 128), BF)],
        (
            core,
            pooled,
            from_left,
            from_right,
            swapped,
            paired,
            sources,
            targets,
            cot_low,
            cot_high,
            bev_cell.reshape(1, voxels),
            head_weight,
            conv_weight.reshape(table_width, 256),
            upstream,
            window,
        ),
        specs=[SMEM] + [VMEM] * 11 + [ANY] * 3,
        out=ANY,
        scratch=[
            pltpu.VMEM((256, 5 * 128), BF),
            pltpu.VMEM((OFFS * 256, 128), BF),
            pltpu.VMEM((voxels, table_width), BF),
            pltpu.VMEM((256, voxels), BF),
            pltpu.VMEM((table_width, 256), BF),
            pltpu.VMEM((voxels, 256), F32),
            pltpu.VMEM((voxels, 9 * 128), BF),
            pltpu.VMEM((voxels, 256), BF),
            pltpu.VMEM((grad_rows, 128), BF),
            pltpu.VMEM((grad_rows, 128), BF),
            pltpu.VMEM((128, 6 * 128), BF),
            pltpu.SemaphoreType.DMA((8,)),
        ],
        flops=8 << 30,
        limit=60,
    )

    both = (keep.astype(F32) + swap(send).astype(F32)).astype(BF)
    both, act = lax.optimization_barrier((both, act))
    shares = exchange(both.reshape(16, grad_rows // 16, 128), PLANE)
    share = jnp.sum(shares.astype(F32), axis=0).astype(BF)
    shares = exchange(jnp.broadcast_to(share[None], (4,) + share.shape), "y")
    share = jnp.sum(shares.astype(F32), axis=0).astype(BF)
    head_keep, head_send = call(
        head_kernel,
        [shape((4 * EDGED, 128), BF), shape((4 * EDGED, 128), BF)],
        (core, bev_cell.reshape(1, voxels), act, head_weight),
        specs=[SMEM, VMEM, VMEM, VMEM],
        scratch=[pltpu.VMEM((3, 256, 384), BF), pltpu.VMEM((66 * 64, 128), F32)],
        flops=4 << 30,
    )
    head = (head_keep.astype(F32) + swap(head_send).astype(F32)).astype(BF)
    mine = exchange(jnp.broadcast_to(share[None], (16,) + share.shape), PLANE).reshape(36, 128, 128)
    total = head[:EDGED].astype(F32)
    for d in (1, 2, 3):
        sent = head[d * EDGED : (d + 1) * EDGED]
        total = total + lax.ppermute(sent, "y", [(i, (i + d) % 4) for i in range(4)]).astype(F32)
    tiles = lax.axis_size(PLANE)
    ends = [(t * layers - 1, t * layers) for t in range(1, tiles)]
    beyond = lax.ppermute(total[512:].astype(BF), ALL, ends + [(j, i) for i, j in ends]).astype(F32)
    layer = lax.axis_index(HEIGHT)
    head_out = jnp.concatenate(
        [
            total[:64] + jnp.where(layer == 0, beyond, 0.0),
            total[64:448],
            total[448:512] + jnp.where(layer == layers - 1, beyond, 0.0),
        ]
    ).astype(BF)
    mine, head_out = lax.optimization_barrier((mine, head_out))
    conv_grad, head_grad = join(mine, swap(mine), core)
    return (head_out.reshape(8, 64, 128), conv_grad, head_grad)


def solution(mesh):
    grid = Mesh(mesh.devices.reshape(4, 4, 4, 2), ALL)
    in_specs = (
        P(ALL, None),
        P(ALL, None),
        P(ALL),
        P(PLANE, HEIGHT, None, None),
        P(PLANE, HEIGHT, None, None),
        P(PLANE, HEIGHT, None, None),
        P(PLANE, HEIGHT, None),
        P(),
        P(),
        P(PLANE, None, None),
    )
    out_specs = (P(ALL, None, None), P(), P())
    return jax.shard_map(local, mesh=grid, in_specs=in_specs, out_specs=out_specs, check_vma=False)
```
